256 devices in a mesh: ctx: 32 (over x, z), tp: 8 (over y, core).
Axes of the slice: x: 4, y: 4, z: 8, core: 2. Of those that a mesh axis runs over, the one named last changes fastest.
Arguments:
- query: bfloat16 [12288, 4096], P('ctx', 'tp'), may hold values from -180 to 180
- key: bfloat16 [12288, 1024], P('ctx', 'tp'), may hold values from -6 to 6
- value: bfloat16 [12288, 1024], P('ctx', 'tp'), may hold values from -6 to 6
- doc_ids: int32 [12288], P('ctx'), may hold values from 0 to 15, as said below
- mamba_x: bfloat16 [12288, 4096], P('ctx', 'tp'), may hold values from -6 to 6
- mamba_bc: bfloat16 [12288, 2, 1024], P('ctx', None, 'tp'), may hold values from -6 to 6
- gate_z: bfloat16 [12288, 4096], P('ctx', 'tp'), may hold values from -6 to 6
- dt_raw: float32 [64, 12288], P('tp', 'ctx'), may hold values from -6 to 5
- decay_rate: float32 [64], P('tp'), may hold values from 1.5318628e-05 to 0.05
- conv_x: float32 [4, 4096], P(None, 'tp'), may hold values from -3 to 3
- conv_bc: float32 [4, 2, 1024], P(None, None, 'tp'), may hold values from -3 to 3
- skip_gain: float32 [64], P('tp'), may hold values from 0.5 to 1.5
- norm_gain: float32 [4096], P('tp'), may hold values from 0.5 to 1.5
- attn_out_weight: bfloat16 [4096, 5120], P('tp'), may hold values from -0.5 to 0.5
- mamba_out_weight: bfloat16 [4096, 5120], P('tp'), may hold values from -0.09375 to 0.09375
Outputs:
- mixed: bfloat16 [12288, 5120], P(('ctx', 'tp'))
The draws below stay inside these ranges and needn't reach their ends.
Inputs may be any that keep to these rules, and one draw needn't show every extreme that they name: `doc_ids`: ids never fall along the sequence; each document is a run of equal ids of at most 6528 tokens, and one holds exactly 6528.
All inputs are finite; a program needn't handle non-finite values.
Results may differ from the reference program's by a relative error of at most 0.019.
Values may be sent and summed in bfloat16 or wider, within the bound.
No kernel may reach another device: no remote copies, remote signals or barrier semaphores. Data moves between devices by JAX's collectives and lax.ppermute only.
A program may use at most 128 MiB of HBM per device.

```python
import math
import jax
import jax.numpy as jnp
from jax import lax

D = 5120
QUERY_HEADS = 32
KEY_VALUE_HEADS = 8
HEAD_WIDTH = 128
MH = 64
P_SIZE = 64
NS = 128
KW = 4
TOK_DEV = 384
PACKED_TOKENS = 12288
GROUPS = 8
DOCS = 16
DOC_MOST = 6528
N_TP = 8


def shared_keys(key):
    base_offset = jnp.clip(jax.random.normal(jax.random.fold_in(key, 101), (PACKED_TOKENS, KEY_VALUE_HEADS * HEAD_WIDTH), jnp.float32), -6.0, 6.0)
    strength = jax.random.uniform(jax.random.fold_in(key, 102), (PACKED_TOKENS, 1), jnp.float32, 10.0, 30.0)
    return (base_offset, strength)


def long_layout(key):
    shard_count = PACKED_TOKENS // TOK_DEV
    first_shard = jax.random.randint(jax.random.fold_in(key, 201), (), 0, shard_count // 2 - 1, dtype=jnp.int32)
    inner_offset = jax.random.randint(jax.random.fold_in(key, 202), (), TOK_DEV // 4, 3 * TOK_DEV // 4, dtype=jnp.int32)
    return (first_shard, inner_offset)


def draw_doc_ids(key, part):
    first_shard, inner_offset = long_layout(key)
    key = jax.random.fold_in(key, 9)
    rest_tokens = PACKED_TOKENS - DOC_MOST
    long_start = (first_shard * TOK_DEV + inner_offset).astype(jnp.int32)
    picked = jax.random.permutation(key, rest_tokens - 2)[:DOCS - 3].astype(jnp.int32) + 1
    other_cuts = jnp.where(picked < long_start, picked, picked + 1).astype(jnp.int32)
    cuts = jnp.concatenate([other_cuts, long_start[None]], axis=0)
    positions = jnp.arange(PACKED_TOKENS, dtype=jnp.int32)
    before = positions < long_start
    after = positions >= long_start + DOC_MOST
    rest_pos = jnp.where(before, positions, jnp.where(after, positions - DOC_MOST, long_start)).astype(jnp.int32)
    rest_id = jnp.sum((cuts[None, :] <= rest_pos[:, None]).astype(jnp.int32), axis=1).astype(jnp.int32)
    return (rest_id + after.astype(jnp.int32)).astype(jnp.int32)


def draw_key(key, part):
    base_offset, strength = shared_keys(key)
    return base_offset.astype(jnp.bfloat16)


def draw_query(key, part):
    base_offset, strength = shared_keys(key)
    first_shard, inner_offset = long_layout(key)
    key = jax.random.fold_in(key, 5)
    drawn = jnp.clip(jax.random.normal(key, (PACKED_TOKENS, QUERY_HEADS * HEAD_WIDTH), jnp.float32), -6.0, 6.0)
    positions = jnp.arange(PACKED_TOKENS, dtype=jnp.int32)
    spread_factor = jnp.repeat(base_offset.reshape(PACKED_TOKENS, KEY_VALUE_HEADS, HEAD_WIDTH), QUERY_HEADS // KEY_VALUE_HEADS, axis=1).reshape(PACKED_TOKENS, QUERY_HEADS * HEAD_WIDTH)
    shard_count = PACKED_TOKENS // TOK_DEV
    long_start = first_shard * TOK_DEV + inner_offset
    last_start = (first_shard + shard_count // 2 + 1) * TOK_DEV
    offsets = positions - last_start
    far_rows = (offsets >= 0) & (offsets < inner_offset)
    target = (long_start + jnp.where(far_rows, offsets, 0) % (TOK_DEV - inner_offset)).astype(jnp.int32)
    far_aligned = spread_factor[target] * strength
    drawn = jnp.where(far_rows[:, None], far_aligned, drawn)
    return drawn.astype(jnp.bfloat16)


def draw_dt_raw(key, part):
    key = jax.random.fold_in(key, 7)
    half_block = TOK_DEV // 2
    block_count = PACKED_TOKENS // half_block
    levels = jax.random.uniform(jax.random.fold_in(key, 1), (MH, block_count), jnp.float32, -4.0, 3.0)
    noise = jnp.clip(0.7 * jax.random.normal(jax.random.fold_in(key, 2), (MH, PACKED_TOKENS), jnp.float32), -2.0, 2.0)
    return (jnp.repeat(levels, half_block, axis=1) + noise).astype(jnp.float32)


def shard_levels(rng, shape, shards, low, top_value):
    def one(axis_at, parts):
        steps = jax.random.uniform(jax.random.fold_in(jax.random.fold_in(rng, 6), axis_at), (parts,), jnp.float32, low / len(shards), top_value / len(shards))
        return jnp.repeat(jnp.exp(steps), shape[axis_at] // parts).reshape((-1,) + (1,) * (len(shape) - axis_at - 1))

    loudness = one(*shards[0])
    for cut in shards[1:]:
        loudness = loudness * one(*cut)
    return loudness


def gaussian(own_key, shape, deviation, reach, shards=(), kind=jnp.bfloat16):
    array = deviation * jax.random.normal(own_key, shape, jnp.float32)
    if shards:
        array = array * shard_levels(own_key, shape, shards, -0.22, 0.18)
    return jnp.clip(array, -reach, reach).astype(kind)


def setup_inputs(seed: int = 0) -> dict:
    key_of = jax.random.split(jax.random.key(seed), 16)
    return {
        "query": draw_query(jax.random.fold_in(key_of[15], 71), 0),
        "key": draw_key(jax.random.fold_in(key_of[15], 71), 0),
        "value": gaussian(key_of[2], (PACKED_TOKENS, KEY_VALUE_HEADS * HEAD_WIDTH), 1.0, 6.0, ((0, 32), (1, 8))),
        "doc_ids": draw_doc_ids(jax.random.fold_in(key_of[15], 71), 0),
        "mamba_x": gaussian(key_of[4], (PACKED_TOKENS, MH * P_SIZE), 1.0, 6.0, ((0, 32), (1, 8))),
        "mamba_bc": gaussian(key_of[5], (PACKED_TOKENS, 2, GROUPS * NS), 1.0, 6.0, ((0, 32), (2, 8))),
        "gate_z": gaussian(key_of[6], (PACKED_TOKENS, MH * P_SIZE), 1.0, 6.0, ((0, 32), (1, 8))),
        "dt_raw": draw_dt_raw(jax.random.fold_in(key_of[15], 71), 0),
        "decay_rate": jnp.clip(jnp.exp(math.log(0.05) - 8.090709 * jax.random.uniform(key_of[8], (MH,), jnp.float32) ** shard_levels(key_of[8], (MH,), ((0, 8),), -0.2, 0.2)), 1.5318628356908448e-05, 0.05),
        "conv_x": gaussian(key_of[9], (KW, MH * P_SIZE), KW ** -0.5, 3.0, ((1, 8),), jnp.float32),
        "conv_bc": gaussian(key_of[10], (KW, 2, GROUPS * NS), KW ** -0.5, 3.0, ((2, 8),), jnp.float32),
        "skip_gain": jnp.clip(0.5 + 1.0 * jax.random.uniform(key_of[11], (MH,), jnp.float32) ** shard_levels(key_of[11], (MH,), ((0, 8),), -0.2, 0.2), 0.5, 1.5),
        "norm_gain": jnp.clip(0.5 + 1.0 * jax.random.uniform(key_of[12], (MH * P_SIZE,), jnp.float32) ** shard_levels(key_of[12], (MH * P_SIZE,), ((0, 8),), -0.2, 0.2), 0.5, 1.5),
        "attn_out_weight": gaussian(key_of[13], (QUERY_HEADS * HEAD_WIDTH, D), HEAD_WIDTH ** -0.5, 0.5, ((0, 8),)),
        "mamba_out_weight": gaussian(key_of[14], (MH * P_SIZE, D), (MH * P_SIZE) ** -0.5, 0.09375, ((0, 8),)),
    }


lowest_score = -1e+30
highest = lax.Precision.HIGHEST

def span_scan(ssm_input, b_rows, c_rows, step_size, log_cum, doc_block, prev_doc, state_in, skip_terms):
    length = doc_block.shape[0]
    order = jnp.arange(length, dtype=jnp.int32)
    allowed = (doc_block[:, None] == doc_block[None, :]) & (order[None, :] <= order[:, None])
    log_gap = log_cum[..., :, None] - log_cum[..., None, :]
    decay = jnp.exp(jnp.where(allowed, log_gap, lowest_score))
    c_dot_b = jnp.einsum('tgn,sgn->gts', c_rows, b_rows, precision=highest)
    mixing = decay * c_dot_b[:, None] * step_size[..., None, :]
    y_intra = jnp.einsum('ghts,sghp->tghp', mixing, ssm_input, precision=highest)
    continues = (doc_block == prev_doc).astype(jnp.float32)
    entry = jnp.exp(jnp.moveaxis(log_cum, -1, 0)) * continues[:, None, None]
    y_state = jnp.einsum('tgn,ghpn->tghp', c_rows, state_in, precision=highest) * entry[..., None]
    output = y_intra + y_state + skip_terms[None, :, :, None] * ssm_input
    last_doc = doc_block[length - 1]
    end_weight = jnp.where(doc_block == last_doc, jnp.exp(log_cum[..., length - 1:] - log_cum), 0.0) * step_size
    state_local = jnp.einsum('ghs,sghp,sgn->ghpn', end_weight, ssm_input, b_rows, precision=highest)
    whole_doc = jnp.logical_and(doc_block[0] == prev_doc, last_doc == doc_block[0]).astype(jnp.float32)
    pass_gain = jnp.exp(log_cum[..., length - 1]) * whole_doc
    return (output, state_local, pass_gain)

def convolve(values, weights, doc_ids):
    padded = jnp.concatenate([jnp.zeros((KW - 1,) + values.shape[1:], jnp.float32), values], axis=0)
    doc_pad = jnp.concatenate([jnp.full((KW - 1,), -1, jnp.int32), doc_ids], axis=0)
    result = jnp.zeros(values.shape, jnp.float32)
    for kernel_tap in range(KW):
        same_doc = (doc_pad[kernel_tap:kernel_tap + PACKED_TOKENS] == doc_ids).astype(jnp.float32)
        same_doc = same_doc.reshape((PACKED_TOKENS,) + (1,) * (values.ndim - 1))
        result = result + weights[kernel_tap] * padded[kernel_tap:kernel_tap + PACKED_TOKENS] * same_doc
    return jax.nn.silu(result).astype(jnp.bfloat16)

def reference(query, key, value, doc_ids, mamba_x, mamba_bc, gate_z, dt_raw, decay_rate, conv_x, conv_bc, skip_gain, norm_gain, attn_out_weight, mamba_out_weight):
    group_width = QUERY_HEADS // KEY_VALUE_HEADS
    block_width = min(512, PACKED_TOKENS)
    window_length = min(DOC_MOST + block_width, PACKED_TOKENS)

    def attend(block_first_row):
        query_block = lax.dynamic_slice_in_dim(query, block_first_row, block_width, 0).astype(jnp.float32).reshape(block_width, KEY_VALUE_HEADS, group_width, HEAD_WIDTH)
        key_first_row = jnp.maximum(block_first_row + block_width - window_length, 0).astype(jnp.int32)
        key_window_rows = lax.dynamic_slice_in_dim(key, key_first_row, window_length, 0).astype(jnp.float32).reshape(window_length, KEY_VALUE_HEADS, HEAD_WIDTH)
        value_window_rows = lax.dynamic_slice_in_dim(value, key_first_row, window_length, 0).astype(jnp.float32).reshape(window_length, KEY_VALUE_HEADS, HEAD_WIDTH)
        q_pos = block_first_row + jnp.arange(block_width, dtype=jnp.int32)
        k_pos = key_first_row + jnp.arange(window_length, dtype=jnp.int32)
        q_doc = lax.dynamic_slice_in_dim(doc_ids, block_first_row, block_width, 0)
        k_doc = lax.dynamic_slice_in_dim(doc_ids, key_first_row, window_length, 0)
        allowed = (k_doc[None, :] == q_doc[:, None]) & (k_pos[None, :] <= q_pos[:, None])
        scores = jnp.einsum('qhgd,khd->hgqk', query_block, key_window_rows) * HEAD_WIDTH ** (-0.5)
        row_max = lax.optimization_barrier(jnp.max(jnp.where(allowed, scores, lowest_score), axis=-1))
        raw = jnp.where(allowed, jnp.exp(scores - row_max[..., None]), 0.0)
        weight_sum = lax.optimization_barrier(jnp.sum(raw, axis=-1))
        rounded = lax.optimization_barrier(raw.astype(jnp.bfloat16)).astype(jnp.float32)
        mixed_values = jnp.einsum('hgqk,khd->hgqd', rounded, value_window_rows)
        result = mixed_values / weight_sum[..., None]
        return result.transpose(2, 0, 1, 3).reshape(block_width, QUERY_HEADS * HEAD_WIDTH).astype(jnp.bfloat16)
    starts = jnp.arange(PACKED_TOKENS // block_width, dtype=jnp.int32) * block_width
    attended = lax.map(attend, starts).reshape(PACKED_TOKENS, QUERY_HEADS * HEAD_WIDTH)
    x_conv = convolve(mamba_x.astype(jnp.float32), conv_x, doc_ids)
    bc_conv = convolve(mamba_bc.astype(jnp.float32), conv_bc, doc_ids)
    per_group = MH // GROUPS
    span = 256 if PACKED_TOKENS % 256 == 0 else PACKED_TOKENS
    n_spans = PACKED_TOKENS // span
    ssm_all = x_conv.astype(jnp.float32).reshape(n_spans, span, GROUPS, per_group, P_SIZE)
    b_all = bc_conv[:, 0].astype(jnp.float32).reshape(n_spans, span, GROUPS, NS)
    c_all = bc_conv[:, 1].astype(jnp.float32).reshape(n_spans, span, GROUPS, NS)
    step_size = jax.nn.softplus(dt_raw)
    log_step = (-step_size * decay_rate[:, None]).reshape(MH, n_spans, span)
    log_cum = jnp.moveaxis(jnp.cumsum(log_step, axis=-1), 1, 0).reshape(n_spans, GROUPS, per_group, span)
    step_all = jnp.moveaxis(step_size.reshape(MH, n_spans, span), 1, 0).reshape(n_spans, GROUPS, per_group, span)
    doc_all = doc_ids.reshape(n_spans, span)
    skip_terms = skip_gain.reshape(GROUPS, per_group)

    def advance(carried, inputs):
        state, prev_doc = carried
        ssm_input, b_rows, c_rows, step_block, cum_block, doc_block = inputs
        output, state_local, pass_gain = span_scan(ssm_input, b_rows, c_rows, step_block, cum_block, doc_block, prev_doc, state, skip_terms)
        return ((pass_gain[..., None, None] * state + state_local, doc_block[span - 1]), output)
    init_state = (jnp.zeros((GROUPS, per_group, P_SIZE, NS), jnp.float32), jnp.int32(-1))
    final_state, ssm_blocks = lax.scan(advance, init_state, (ssm_all, b_all, c_all, step_all, log_cum, doc_all))
    ssm_out = ssm_blocks.reshape(PACKED_TOKENS, MH * P_SIZE)
    gated = ssm_out * jax.nn.silu(gate_z.astype(jnp.float32))
    grouped = gated.reshape(PACKED_TOKENS, GROUPS, -1)
    inverse = lax.rsqrt(lax.optimization_barrier(jnp.mean(grouped * grouped, axis=-1, keepdims=True)) + 1e-05)
    normed = ((grouped * inverse).reshape(PACKED_TOKENS, MH * P_SIZE) * norm_gain).astype(jnp.bfloat16)
    attn_cols = QUERY_HEADS * HEAD_WIDTH // N_TP
    ssm_cols = MH * P_SIZE // N_TP
    mixed = jnp.zeros((PACKED_TOKENS, D), jnp.float32)
    for part_index in range(N_TP):
        left = jnp.dot(attended[:, part_index * attn_cols:(part_index + 1) * attn_cols], attn_out_weight[part_index * attn_cols:(part_index + 1) * attn_cols], preferred_element_type=jnp.float32)
        right = jnp.dot(normed[:, part_index * ssm_cols:(part_index + 1) * ssm_cols], mamba_out_weight[part_index * ssm_cols:(part_index + 1) * ssm_cols], preferred_element_type=jnp.float32)
        partial_sum = lax.optimization_barrier((left + right).astype(jnp.bfloat16)).astype(jnp.float32)
        mixed = mixed + partial_sum
    return mixed.astype(jnp.bfloat16)
```

```python
import functools
import math

import jax
import jax.numpy as jnp
from jax import lax
from jax.experimental import pallas as pl
from jax.experimental.pallas import tpu as pltpu
from jax.sharding import PartitionSpec as P

T = 384
HW = 128
QH = 4
MHL = 8
PS = 64
NS = 128
KW = 4
D = 5120
ROWS = T + 16
LOW = -1e30
SCALE = HW**-0.5 * math.log2(math.e)
f32 = jnp.float32
bf16 = jnp.bfloat16

VMEM = pl.BlockSpec(memory_space=pltpu.VMEM)
SMEM = pl.BlockSpec(memory_space=pltpu.SMEM)


def params(mib):
    return pltpu.CompilerParams(vmem_limit_bytes=mib * 2**20)


def cost(flops, nbytes, trans=0):
    return pl.CostEstimate(flops=int(flops), bytes_accessed=int(nbytes), transcendentals=int(trans))


def sds(shape, dtype):
    return jax.ShapeDtypeStruct(shape, dtype)


def nt(a, b):
    return lax.dot_general(a, b, (((1,), (1,)), ((), ())), preferred_element_type=f32)


def nn(a, b):
    return lax.dot_general(a, b, (((1,), (0,)), ((), ())), preferred_element_type=f32)


def column_of(row):
    return jnp.transpose(jnp.broadcast_to(row, (128, T)))


def columns_of(rows):
    return jnp.transpose(jnp.concatenate([rows, jnp.zeros((120, T), f32)], axis=0))


def tile_lanes(a, n):
    return jnp.concatenate([a] * n, axis=1)


def local_kernel(
    doc_s, rate_s, x_ref, bc_ref, tail_ref, doc_ref, dt_ref, cx_ref, cbc_ref,
    xc_ref, bcc_ref, cs_ref, msg_ref, ext_ref, dex_ref,
):
    own = column_of(doc_ref[...].astype(f32) + 1.0)
    tail = tail_ref[...].astype(f32)
    ext_ref[:16, :] = tail[:, :768]
    ext_ref[16:, :512] = x_ref[...].astype(f32)
    ext_ref[16:, 512:] = bc_ref[...].astype(f32)
    dex_ref[:16, :] = tail[:, 768:]
    dex_ref[16:, :] = own
    for r in range(0, T, 128):
        acc = [jnp.zeros((128, 128), f32) for _ in range(6)]
        for k in range(KW):
            lo = r + 13 + k
            same = (dex_ref[lo : lo + 128, :] == dex_ref[r + 16 : r + 144, :]).astype(f32)
            for c in range(6):
                w = cx_ref[k : k + 1, c * 128 : c * 128 + 128] if c < 4 else (
                    cbc_ref[k : k + 1, (c - 4) * 128 : (c - 4) * 128 + 128]
                )
                acc[c] = acc[c] + w * ext_ref[lo : lo + 128, c * 128 : c * 128 + 128] * same
        for c in range(6):
            v = jax.nn.silu(acc[c]).astype(bf16)
            if c < 4:
                xc_ref[r : r + 128, c * 128 : c * 128 + 128] = v
            else:
                bcc_ref[r : r + 128, (c - 4) * 128 : (c - 4) * 128 + 128] = v
    dt = dt_ref[...]
    step = jnp.maximum(dt, 0.0) + jnp.log1p(jnp.exp(-jnp.abs(dt)))
    head = lax.broadcasted_iota(jnp.int32, (MHL, T), 0)
    rate = jnp.zeros((MHL, T), f32)
    for h in range(MHL):
        rate = jnp.where(head == h, rate_s[h], rate)
    tri = (
        lax.broadcasted_iota(jnp.int32, (T, T), 0) <= lax.broadcasted_iota(jnp.int32, (T, T), 1)
    ).astype(f32)
    cum = lax.dot_general(
        -step * rate, tri, (((1,), (0,)), ((), ())),
        precision=lax.Precision.HIGHEST, preferred_element_type=f32,
    )
    cs_ref[:8, :] = cum
    cs_ref[8:, :] = step
    cum_end = cum[:, T - 1 :]
    end_w = jnp.where(doc_ref[...] == doc_s[T - 1], jnp.exp(cum_end - cum) * step, 0.0)
    xt = jnp.transpose(xc_ref[...].astype(f32))
    xw = (xt.reshape(MHL, PS, T) * end_w[:, None, :]).reshape(MHL * PS, T).astype(bf16)
    state = nn(xw, bcc_ref[:, :NS])
    msg_ref[:, :16, :] = state.astype(bf16).reshape(32, 16, NS)
    first = doc_s[0]
    whole = jnp.logical_and(
        tail[15:16, 768:] == first.astype(f32) + 1.0, doc_s[T - 1] == first
    ).astype(f32)
    gain = jnp.exp(cum_end) * whole
    high = gain.astype(bf16).astype(f32)
    low = gain - high
    row = lax.broadcasted_iota(jnp.int32, (MHL, 16, NS), 1)
    block = jnp.where(
        row == 0, high[:, None, :], jnp.where(row == 1, low[:, None, :], 0.0)
    ).astype(bf16)
    for q in range(4):
        for h in range(MHL):
            msg_ref[h * 4 + q, 16:, :] = block[h]


def scan_kernel(msg_ref, out_ref):
    state = jnp.zeros((16, NS), f32)
    for j in range(32):
        out_ref[j] = state.astype(bf16)
        block = msg_ref[j].astype(f32)
        state = (block[16:17] + block[17:18]) * state + block[:16]


def intra_kernel(skip_s, xc_ref, bcc_ref, cs_ref, doc_ref, y_ref, cb_ref):
    row = doc_ref[...].astype(f32)
    own = column_of(row)
    order_t = lax.broadcasted_iota(jnp.int32, (T, T), 0)
    order_s = lax.broadcasted_iota(jnp.int32, (T, T), 1)
    allowed = (tile_lanes(own, 3) == row) & (order_s <= order_t)
    cb_ref[...] = jnp.where(allowed, nt(bcc_ref[:, NS:], bcc_ref[:, :NS]), 0.0)
    cum = cs_ref[:8, :]
    cum_t = columns_of(cum)
    late = cum - jnp.log(cs_ref[8:, :])
    for r in range(0, T, 128):
        k = r + 128
        cb = cb_ref[r:k, :k]
        for pair in range(MHL // 2):
            halves = []
            for h in (2 * pair, 2 * pair + 1):
                gap = cum_t[r:k, h : h + 1] - late[h : h + 1, :k]
                mix = (jnp.exp(jnp.minimum(gap, 60.0)) * cb).astype(bf16)
                x = xc_ref[:k, h * PS : (h + 1) * PS]
                halves.append(nn(mix, x) + skip_s[h] * x[r:k].astype(f32))
            y_ref[r:k, pair * 128 : pair * 128 + 128] = jnp.concatenate(halves, axis=1)


def deal_rows(pos_s, full_ref, send_ref, keep_ref):
    tp = pos_s[1]
    core = lax.rem(tp, 2)
    for d in range(4):
        base = 2 * lax.rem(tp // 2 + d, 4)
        mine = pl.multiple_of((base + core) * 48, 16)
        other = pl.multiple_of((base + 1 - core) * 48, 16)
        keep_ref[d * 48 : d * 48 + 48, :] = full_ref[pl.ds(mine, 48), :]
        send_ref[d * 48 : d * 48 + 48, :] = full_ref[pl.ds(other, 48), :]


def gated_kernel(
    pos_s, y_ref, state_ref, bcc_ref, cs_ref, doc_ref, tail_ref, z_ref, gain_ref,
    send_ref, keep_ref, full_ref, g_ref,
):
    own = column_of(doc_ref[...].astype(f32) + 1.0)
    prev = tail_ref[15:16, 768:].astype(f32)
    entry = jnp.exp(columns_of(cs_ref[:8, :])) * (own == prev).astype(f32)
    from_state = nt(bcc_ref[:, NS:], state_ref[...])
    lane = lax.broadcasted_iota(jnp.int32, (T, 128), 1)
    total = jnp.zeros((T, 1), f32)
    for pair in range(MHL // 2):
        c = slice(pair * 128, pair * 128 + 128)
        e = jnp.where(
            lane < PS, entry[:, 2 * pair : 2 * pair + 1], entry[:, 2 * pair + 1 : 2 * pair + 2]
        )
        g = (y_ref[:, c] + from_state[:, c] * e) * jax.nn.silu(z_ref[:, c].astype(f32))
        g_ref[:, c] = g
        total = total + jnp.sum(g * g, axis=1, keepdims=True)
    inverse = lax.rsqrt(total * (1.0 / (MHL * PS)) + 1e-05)
    full_ref[...] = (g_ref[...] * inverse * gain_ref[...]).astype(bf16)
    deal_rows(pos_s, full_ref, send_ref, keep_ref)


def fold(s, values, m_ref, al_ref, h):
    m_old = m_ref[h]
    m_new = jnp.maximum(m_old, jnp.max(s, axis=1, keepdims=True))
    p = jnp.exp2((s - tile_lanes(m_new, s.shape[1] // 128)) * SCALE)
    factor = jnp.exp2((m_old - m_new) * SCALE)
    al_ref[h] = al_ref[h] * tile_lanes(factor, 2) + nn(p.astype(bf16), values)
    m_ref[h] = m_new


def with_ones(v):
    return jnp.concatenate([v, jnp.ones(v.shape, bf16)], axis=1)


def own_kernel(q_ref, k_ref, v_ref, doc_ref, m_ref, al_ref):
    row = doc_ref[...].astype(f32)
    own = column_of(row)
    order_t = lax.broadcasted_iota(jnp.int32, (T, T), 0)
    order_s = lax.broadcasted_iota(jnp.int32, (T, T), 1)
    allowed = (tile_lanes(own, 3) == row) & (order_s <= order_t)
    k = k_ref[...]
    values = with_ones(v_ref[...])
    for h in range(QH):
        s = jnp.where(allowed, nt(q_ref[:, h * HW : (h + 1) * HW], k), LOW)
        m = jnp.broadcast_to(jnp.max(s, axis=1, keepdims=True), (T, 128))
        p = jnp.exp2((s - tile_lanes(m, 3)) * SCALE)
        al_ref[h] = nn(p.astype(bf16), values)
        m_ref[h] = m


def wave(blocks, pos_s, doc_s, q_ref, pack_refs, doc_ref, m_in, al_in, m_ref, al_ref):
    m_ref[...] = m_in[...]
    al_ref[...] = al_in[...]
    first = doc_s[0].astype(f32)
    for which, base, behind in blocks:
        ref = pack_refs[which]
        ids = ref[base + T : base + ROWS, :].astype(f32)
        ids = jnp.concatenate([ids[:1, :], ids[1:2, :128]], axis=1)
        touches = (jnp.max(ids) == first) & (pos_s[0] >= behind)
        whole = jnp.min(ids) == first

        @pl.when(touches & whole)
        def _():
            k = ref[base : base + T, :HW]
            values = with_ones(ref[base : base + T, HW:])
            for h in range(QH):
                fold(nt(q_ref[:, h * HW : (h + 1) * HW], k), values, m_ref, al_ref, h)

        @pl.when(touches & jnp.logical_not(whole))
        def _():
            k = ref[base : base + T, :HW]
            values = with_ones(ref[base : base + T, HW:])
            bias = jnp.where(ids == first, 0.0, LOW)

            @pl.loop(0, QH)
            def _(h):
                q = q_ref[:, pl.ds(pl.multiple_of(h * HW, HW), HW)]
                fold(nt(q, k) + bias, values, m_ref, al_ref, h)

    @pl.when(doc_s[T - 1] != doc_s[0])
    def _():
        keeps = column_of(doc_ref[...].astype(f32)) == first

        @pl.loop(0, QH)
        def _(h):
            m_ref[h] = jnp.where(keeps, m_ref[h], m_in[h])
            al_ref[h] = jnp.where(tile_lanes(keeps, 2), al_ref[h], al_in[h])


def wave_kernel(blocks, n, pos_s, doc_s, q_ref, *refs):
    doc_ref, m_in, al_in, m_ref, al_ref = refs[n:]
    wave(blocks, pos_s, doc_s, q_ref, refs[:n], doc_ref, m_in, al_in, m_ref, al_ref)


def last_wave_kernel(blocks, n, pos_s, doc_s, q_ref, *refs):
    doc_ref, m_in, al_in, send_ref, keep_ref, m_ref, al_ref, full_ref = refs[n:]
    wave(blocks, pos_s, doc_s, q_ref, refs[:n], doc_ref, m_in, al_in, m_ref, al_ref)
    for h in range(QH):
        full_ref[:, h * HW : (h + 1) * HW] = (
            al_ref[h, :, :HW] / al_ref[h, :, HW:]
        ).astype(bf16)
    deal_rows(pos_s, full_ref, send_ref, keep_ref)


STATE = [sds((QH, T, 128), f32), sds((QH, T, 256), f32)]


def attend_own(q, k, v, doc_row):
    return pl.pallas_call(
        own_kernel,
        out_shape=STATE,
        in_specs=[VMEM] * 4,
        out_specs=[VMEM] * 2,
        compiler_params=params(32),
        cost_estimate=cost(2e9, 4e6, 6e5),
        name="own",
    )(q, k, v, doc_row)


def attend_wave(blocks, pos, docs, q, packs, doc_row, state, last=False):
    n = len(packs)
    args = (pos, docs, q, *packs, doc_row, *state)
    specs = [SMEM, SMEM] + [VMEM] * (n + 4)
    common = dict(
        in_specs=specs,
        compiler_params=params(40),
        cost_estimate=cost(1.2e9 * len(blocks), 4e6 * len(blocks), 6e5 * len(blocks)),
    )
    if last:
        half = sds((T // 2, QH * HW), bf16)
        return pl.pallas_call(
            functools.partial(last_wave_kernel, blocks, n),
            out_shape=[half, half],
            out_specs=[VMEM] * 2,
            scratch_shapes=[
                pltpu.VMEM((QH, T, 128), f32),
                pltpu.VMEM((QH, T, 256), f32),
                pltpu.VMEM((T, QH * HW), bf16),
            ],
            name="last_wave",
            **common,
        )(*args)
    return pl.pallas_call(
        functools.partial(wave_kernel, blocks, n),
        out_shape=STATE,
        out_specs=[VMEM] * 2,
        name="wave",
        **common,
    )(*args)


def project_kernel(keep_ref, got_ref, own_ref, other_ref, out_ref):
    out_ref[...] = nn(keep_ref[...], own_ref[...]) + nn(got_ref[...], other_ref[...])


def project(keep, got, w_own, w_other):
    cols = 512
    rows, depth = keep.shape
    wide = pl.BlockSpec((depth, cols), lambda j: (0, j))
    whole = pl.BlockSpec((rows, depth), lambda j: (0, 0))
    return pl.pallas_call(
        project_kernel,
        grid=(D // cols,),
        out_shape=sds((rows, D), f32),
        in_specs=[whole, whole, wide, wide],
        out_specs=pl.BlockSpec((rows, cols), lambda j: (0, j)),
        compiler_params=params(16),
        cost_estimate=cost(2e9, 15e6),
        name="project",
    )(keep, got, w_own, w_other)


def combine_kernel(keep_ref, got_ref, own_ref, other_ref, add_ref, *outs):
    total = nn(keep_ref[...], own_ref[...]) + nn(got_ref[...], other_ref[...]) + add_ref[...]
    for d in range(4):
        outs[d][...] = total[d * 48 : d * 48 + 48].astype(outs[d].dtype)


def combine(keep, got, w_own, w_other, add, half):
    cols = 512
    rows, depth = keep.shape
    steps = D // cols // 2
    wide = pl.BlockSpec((depth, cols), lambda j: (0, j + half * steps))
    whole = pl.BlockSpec((rows, depth), lambda j: (0, 0))
    piece = pl.BlockSpec((48, cols), lambda j: (0, j))
    return pl.pallas_call(
        combine_kernel,
        grid=(steps,),
        out_shape=[sds((48, D // 2), t) for t in (f32, bf16, bf16, bf16)],
        in_specs=[whole, whole, wide, wide, pl.BlockSpec((rows, cols), lambda j: (0, j + half * steps))],
        out_specs=[piece] * 4,
        compiler_params=params(16),
        cost_estimate=cost(1e9, 8e6),
        name="combine",
    )(keep, got, w_own, w_other, add)


def along(v, by):
    n = lax.axis_size("ctx")
    return lax.ppermute(v, "ctx", [(i, (i + by) % n) for i in range(n)])


def from_previous(v):
    n = lax.axis_size("ctx")
    return lax.ppermute(v, "ctx", [(i, i + 1) for i in range(n - 1)])


def along_y(v, by):
    return lax.ppermute(
        v, "tp", [(2 * y + c, 2 * ((y + by) % 4) + c) for y in range(4) for c in range(2)]
    )


def other_core(v):
    return lax.ppermute(v, "tp", [(i, i ^ 1) for i in range(8)])


def body(
    query, key, value, doc_ids, mamba_x, mamba_bc, gate_z, dt_raw, decay_rate,
    conv_x, conv_bc, skip_gain, norm_gain, attn_out_weight, mamba_out_weight,
):
    pos = jnp.stack([lax.axis_index("ctx"), lax.axis_index("tp")]).astype(jnp.int32)
    doc_row = doc_ids.reshape(1, T)
    bc = mamba_bc.reshape(T, 2 * NS)

    tail = from_previous(
        jnp.concatenate(
            [
                mamba_x[T - 16 :],
                bc[T - 16 :],
                jnp.broadcast_to((doc_ids[T - 16 :] + 1).astype(bf16)[:, None], (16, 128)),
            ],
            axis=1,
        )
    )

    ids = jnp.pad(doc_ids.astype(bf16), (0, 128)).reshape(2, 256)
    pack = jnp.concatenate(
        [jnp.concatenate([key, value], axis=1), jnp.pad(ids, ((0, 14), (0, 0)))], axis=0
    )
    g1 = along(pack, 1)
    g8 = along(pack, 8)
    g16 = along(pack, 16)

    attn_other = other_core(attn_out_weight)
    mamba_other = other_core(mamba_out_weight)

    state = attend_own(query, key, value, doc_row)

    xc, bcc, cs, msg = pl.pallas_call(
        local_kernel,
        out_shape=[
            sds((T, MHL * PS), bf16),
            sds((T, 2 * NS), bf16),
            sds((16, T), f32),
            sds((32, 32, NS), bf16),
        ],
        in_specs=[SMEM, SMEM] + [VMEM] * 7,
        out_specs=[VMEM] * 4,
        scratch_shapes=[pltpu.VMEM((ROWS, 768), f32), pltpu.VMEM((ROWS, 128), f32)],
        compiler_params=params(32),
        cost_estimate=cost(1e9, 6e6, 1e6),
        name="local",
    )(doc_ids, decay_rate, mamba_x, bc, tail, doc_row, dt_raw, conv_x, conv_bc.reshape(KW, 2 * NS))

    msg = lax.all_to_all(msg.reshape(32 * 32, NS), "ctx", 0, 0, tiled=True)

    c29 = along(jnp.concatenate([g1, g8], axis=0), 1)
    c715 = along(jnp.concatenate([g8, g16], axis=0), -1)
    g17 = along(g1, 16)

    y = pl.pallas_call(
        intra_kernel,
        out_shape=sds((T, MHL * PS), f32),
        in_specs=[SMEM] + [VMEM] * 4,
        out_specs=VMEM,
        scratch_shapes=[pltpu.VMEM((T, T), f32)],
        compiler_params=params(32),
        cost_estimate=cost(2e9, 4e6, 1e6),
        name="intra",
    )(skip_gain, xc, bcc, cs, doc_row)

    state = attend_wave([(0, 0, 1), (1, 0, 8), (2, 0, 16)], pos, doc_ids, query, [g1, g8, g16], doc_row, state)

    carried = pl.pallas_call(
        scan_kernel,
        out_shape=sds((32, 16, NS), bf16),
        in_specs=[VMEM],
        out_specs=VMEM,
        cost_estimate=cost(1e6, 6e5),
        name="scan",
    )(msg.reshape(32, 32, NS))
    carried = lax.all_to_all(carried.reshape(32 * 16, NS), "ctx", 0, 0, tiled=True)

    c310 = along(c29, 1)
    c614 = along(c715, -1)
    state = attend_wave(
        [(0, 0, 2), (0, ROWS, 9), (1, 0, 7), (1, ROWS, 15), (2, 0, 17)],
        pos, doc_ids, query, [c29, c715, g17], doc_row, state,
    )
    c411 = along(c310, 1)
    c513 = along(c614, -1)
    g12 = along(c310[:ROWS], 9)

    half = sds((T // 2, MHL * PS), bf16)
    normed_send, normed_keep = pl.pallas_call(
        gated_kernel,
        out_shape=[half, half],
        in_specs=[SMEM] + [VMEM] * 8,
        out_specs=[VMEM] * 2,
        scratch_shapes=[pltpu.VMEM((T, MHL * PS), bf16), pltpu.VMEM((T, MHL * PS), f32)],
        compiler_params=params(32),
        cost_estimate=cost(2e9, 4e6, 1e6),
        name="gated",
    )(pos, y, carried, bcc, cs, doc_row, tail, gate_z, norm_gain.reshape(1, MHL * PS))
    normed_got = other_core(normed_send)

    state = attend_wave(
        [(0, 0, 3), (0, ROWS, 10), (1, 0, 6), (1, ROWS, 14)],
        pos, doc_ids, query, [c310, c614], doc_row, state,
    )
    from_mamba = project(normed_keep, normed_got, mamba_out_weight, mamba_other)
    attn_send, attn_keep = attend_wave(
        [(0, 0, 4), (0, ROWS, 11), (1, 0, 5), (1, ROWS, 13), (2, 0, 12)],
        pos, doc_ids, query, [c411, c513, g12], doc_row, state, last=True,
    )
    attn_got = other_core(attn_send)

    own_a, up_a, far_a, down_a = combine(attn_keep, attn_got, attn_out_weight, attn_other, from_mamba, 0)
    own_b, up_b, far_b, down_b = combine(attn_keep, attn_got, attn_out_weight, attn_other, from_mamba, 1)
    far_a = along_y(far_a, 1)
    far_b = along_y(far_b, -1)
    down_a = along_y(down_a, -1)
    up_b = along_y(up_b, 1)
    up_a = along_y((up_a.astype(f32) + far_a.astype(f32)).astype(bf16), 1)
    down_b = along_y((down_b.astype(f32) + far_b.astype(f32)).astype(bf16), -1)
    return jnp.concatenate(
        [
            (own_a + up_a.astype(f32) + down_a.astype(f32)).astype(bf16),
            (own_b + up_b.astype(f32) + down_b.astype(f32)).astype(bf16),
        ],
        axis=1,
    )


def solution(mesh):
    return jax.shard_map(
        body,
        mesh=mesh,
        in_specs=(
            P("ctx", "tp"), P("ctx", "tp"), P("ctx", "tp"), P("ctx"), P("ctx", "tp"),
            P("ctx", None, "tp"), P("ctx", "tp"), P("tp", "ctx"), P("tp"), P(None, "tp"),
            P(None, None, "tp"), P("tp"), P("tp"), P("tp", None), P("tp", None),
        ),
        out_specs=P(("ctx", "tp"), None),
        check_vma=False,
    )
```

```python
import functools
import math

import jax
import jax.numpy as jnp
from jax import lax
from jax.experimental import pallas as pl
from jax.experimental.pallas import tpu as pltpu
from jax.sharding import PartitionSpec as P

T = 384
HW = 128
QH = 4
MHL = 8
PS = 64
NS = 128
KW = 4
D = 5120
COLS = 512
ROWS = 2 * HW + 16
LOW = -1e30
SCALE = HW**-0.5 * math.log2(math.e)
f32 = jnp.float32
bf16 = jnp.bfloat16

VMEM = pl.BlockSpec(memory_space=pltpu.VMEM)
ANY = pl.BlockSpec(memory_space=pl.ANY)
HBM = pl.BlockSpec(memory_space=pltpu.HBM)


def params(mib):
    return pltpu.CompilerParams(vmem_limit_bytes=mib * 2**20)


def cost(flops, nbytes, trans=0):
    return pl.CostEstimate(flops=int(flops), bytes_accessed=int(nbytes), transcendentals=int(trans))


COSTS = {
    "tail": (1e6, 1e4),
    "pack": (1e6, 1e4),
    "local": (1e6, 1e4),
    "join": (1e6, 1e4),
    "tie": (1e6, 1e4),
    "intra": (5e10, 1e6),
    "scan": (1e6, 1e4),
    "attend_first": (5e10, 1e6),
    "gated": (1e6, 1e4),
    "attend_last": (1e6, 1e4),
    "combine": (1e6, 1e4),
}


def sds(shape, dtype):
    return jax.ShapeDtypeStruct(shape, dtype)


def nt(a, b):
    return lax.dot_general(a, b, (((1,), (1,)), ((), ())), preferred_element_type=f32)


def nn(a, b):
    return lax.dot_general(a, b, (((1,), (0,)), ((), ())), preferred_element_type=f32)


def column_of(row):
    return jnp.transpose(jnp.broadcast_to(row, (128, T)))


def columns_of(rows):
    return jnp.transpose(jnp.concatenate([rows, jnp.zeros((120, T), f32)], axis=0))


def column_of_eight(ref):
    row = jnp.broadcast_to(ref[...].reshape(1, 8), (8, 8))
    same = lax.broadcasted_iota(jnp.int32, (8, 8), 0) == lax.broadcasted_iota(jnp.int32, (8, 8), 1)
    return jnp.sum(jnp.where(same, row, 0.0), axis=1, keepdims=True)


def fetch(pairs, sems):
    copies = [pltpu.make_async_copy(a, b, sems.at[i]) for i, (a, b) in enumerate(pairs)]
    for copy in copies:
        copy.start()
    return copies


def tile_lanes(a, n):
    return jnp.concatenate([a] * n, axis=1)


def local_kernel(
    x_hbm, dt_hbm, cx_hbm, rate_hbm, bc_ref, tail_ref, doc_ref, cbc_ref,
    xc_ref, bcc_ref, cs_ref, msg_ref, ext_ref, dex_ref, x_ref, dt_ref, cx_ref, rate_ref, sems,
):
    copies = fetch(
        [(x_hbm, x_ref), (dt_hbm, dt_ref), (cx_hbm, cx_ref), (rate_hbm, rate_ref)], sems
    )
    own = column_of(doc_ref[...].reshape(1, T).astype(f32) + 1.0)
    tail = tail_ref[...].astype(f32)
    ext_ref[:16, :] = tail[:, :768]
    ext_ref[16:, 512:] = bc_ref[...].astype(f32)
    dex_ref[:16, :] = tail[:, 768:]
    dex_ref[16:, :] = own
    for copy in copies:
        copy.wait()
    ext_ref[16:, :512] = x_ref[...].astype(f32)
    for r in range(0, T, 128):
        acc = [jnp.zeros((128, 128), f32) for _ in range(6)]
        for k in range(KW):
            lo = r + 13 + k
            same = (dex_ref[lo : lo + 128, :] == dex_ref[r + 16 : r + 144, :]).astype(f32)
            for c in range(6):
                w = cx_ref[k : k + 1, c * 128 : c * 128 + 128] if c < 4 else (
                    cbc_ref[k : k + 1, (c - 4) * 128 : (c - 4) * 128 + 128]
                )
                acc[c] = acc[c] + w * ext_ref[lo : lo + 128, c * 128 : c * 128 + 128] * same
        for c in range(6):
            v = jax.nn.silu(acc[c]).astype(bf16)
            if c < 4:
                xc_ref[r : r + 128, c * 128 : c * 128 + 128] = v
            else:
                bcc_ref[r : r + 128, (c - 4) * 128 : (c - 4) * 128 + 128] = v
    dt = dt_ref[...]
    step = jnp.maximum(dt, 0.0) + jnp.log1p(jnp.exp(-jnp.abs(dt)))
    rate = column_of_eight(rate_ref)
    tri = (
        lax.broadcasted_iota(jnp.int32, (T, T), 0) <= lax.broadcasted_iota(jnp.int32, (T, T), 1)
    ).astype(f32)
    cum = lax.dot_general(
        -step * rate, tri, (((1,), (0,)), ((), ())),
        precision=lax.Precision.HIGHEST, preferred_element_type=f32,
    )
    cs_ref[:8, :] = cum
    cs_ref[8:, :] = step

    row = doc_ref[...].reshape(1, T).astype(f32)
    first, last = jnp.min(row), jnp.max(row)
    cum_end = cum[:, T - 1 :]
    end_w = jnp.where(row == last, jnp.exp(cum_end - cum) * step, 0.0)
    xt = jnp.transpose(xc_ref[...].astype(f32))
    xw = (xt.reshape(MHL, PS, T) * end_w[:, None, :]).reshape(MHL * PS, T).astype(bf16)
    state = nn(xw, bcc_ref[:, :NS])
    msg_ref[:, :16, :] = state.astype(bf16).reshape(32, 16, NS)
    whole = jnp.logical_and(tail_ref[15:16, 768:].astype(f32) == first + 1.0, last == first).astype(f32)
    gain = jnp.exp(cum_end) * whole
    high = gain.astype(bf16).astype(f32)
    low = gain - high
    at = lax.broadcasted_iota(jnp.int32, (MHL, 16, NS), 1)
    block = jnp.where(
        at == 0, high[:, None, :], jnp.where(at == 1, low[:, None, :], 0.0)
    ).astype(bf16)
    for q in range(4):
        for h in range(MHL):
            msg_ref[h * 4 + q, 16:, :] = block[h]


def scan_kernel(msg_ref, _, out_ref):
    state = jnp.zeros((16, NS), f32)
    for j in range(32):
        out_ref[j] = state.astype(bf16)
        block = msg_ref[j].astype(f32)
        state = (block[16:17] + block[17:18]) * state + block[:16]


def intra_kernel(xc_ref, bcc_ref, cs_ref, doc_ref, skip_ref, *refs):
    y_ref, cb_ref = refs[-2:]
    skip = column_of_eight(skip_ref)
    row = doc_ref[...].reshape(1, T).astype(f32)
    own = column_of(row)
    order_t = lax.broadcasted_iota(jnp.int32, (T, T), 0)
    order_s = lax.broadcasted_iota(jnp.int32, (T, T), 1)
    allowed = (tile_lanes(own, 3) == row) & (order_s <= order_t)
    cb_ref[...] = jnp.where(allowed, nt(bcc_ref[:, NS:], bcc_ref[:, :NS]), 0.0)
    cum = cs_ref[:8, :]
    cum_t = columns_of(cum)
    late = cum - jnp.log(cs_ref[8:, :])
    for r in range(0, T, 128):
        k = r + 128
        cb = cb_ref[r:k, :k]
        for pair in range(MHL // 2):
            halves = []
            for h in (2 * pair, 2 * pair + 1):
                gap = cum_t[r:k, h : h + 1] - late[h : h + 1, :k]
                mix = (jnp.exp(jnp.minimum(gap, 60.0)) * cb).astype(bf16)
                x = xc_ref[:k, h * PS : (h + 1) * PS]
                halves.append(nn(mix, x) + skip[h : h + 1] * x[r:k].astype(f32))
            y_ref[r:k, pair * 128 : pair * 128 + 128] = jnp.concatenate(halves, axis=1)


def deal_rows(full_ref, out_ref):
    tp = lax.axis_index("tp")
    core = lax.rem(tp, 2)
    for d in range(4):
        base = 2 * lax.rem(tp // 2 + d, 4)
        mine = pl.multiple_of((base + core) * 48, 16)
        other = pl.multiple_of((base + 1 - core) * 48, 16)
        out_ref[d * 48 : d * 48 + 48, :] = full_ref[pl.ds(mine, 48), :]
        out_ref[192 + d * 48 : 240 + d * 48, :] = full_ref[pl.ds(other, 48), :]


def gated_kernel(
    z_hbm, y_ref, state_ref, bcc_ref, cs_ref, doc_ref, tail_ref, gain_ref, _,
    out_ref, full_ref, g_ref, z_ref, sems,
):
    copies = fetch([(z_hbm, z_ref)], sems)
    own = column_of(doc_ref[...].reshape(1, T).astype(f32) + 1.0)
    prev = tail_ref[15:16, 768:].astype(f32)
    entry = jnp.exp(columns_of(cs_ref[:8, :])) * (own == prev).astype(f32)
    from_state = nt(bcc_ref[:, NS:], state_ref[...])
    lane = lax.broadcasted_iota(jnp.int32, (T, 128), 1)
    copies[0].wait()
    total = jnp.zeros((T, 1), f32)
    for pair in range(MHL // 2):
        c = slice(pair * 128, pair * 128 + 128)
        e = jnp.where(
            lane < PS, entry[:, 2 * pair : 2 * pair + 1], entry[:, 2 * pair + 1 : 2 * pair + 2]
        )
        g = (y_ref[:, c] + from_state[:, c] * e) * jax.nn.silu(z_ref[:, c].astype(f32))
        g_ref[:, c] = g
        total = total + jnp.sum(g * g, axis=1, keepdims=True)
    inverse = lax.rsqrt(total * (1.0 / (MHL * PS)) + 1e-05)
    full_ref[...] = (g_ref[...] * inverse * gain_ref[...]).astype(bf16)
    deal_rows(full_ref, out_ref)


def tail_kernel(x_ref, bc_ref, doc_ref, tail_ref):
    tail_ref[:, :512] = x_ref[...]
    tail_ref[:, 512:768] = bc_ref[...]
    tail_ref[:, 768:] = (column_of(doc_ref[...].reshape(1, T).astype(f32))[T - 16 :] + 1.0).astype(bf16)


def pack_kernel(k_hbm, v_hbm, doc_ref, _, pack_ref, k_ref, v_ref, sems):
    copies = fetch([(k_hbm, k_ref), (v_hbm, v_ref)], sems)
    row = doc_ref[...].reshape(1, T).astype(f32)
    pack_ref[2 * HW :, :] = jnp.broadcast_to(row, (16, T)).astype(bf16)
    for copy in copies:
        copy.wait()
    pack_ref[:HW, :] = jnp.transpose(k_ref[...].astype(f32)).astype(bf16)
    for c in range(3):
        pack_ref[HW : 2 * HW, c * 128 : c * 128 + 128] = v_ref[c * 128 : c * 128 + 128, :]


def join_kernel(a_ref, b_ref, c_ref, msg_ref, up_ref, down_ref, out_ref):
    up_ref[:ROWS] = a_ref[...]
    up_ref[ROWS:] = b_ref[...]
    down_ref[:ROWS] = b_ref[...]
    down_ref[ROWS:] = c_ref[...]
    out_ref[...] = msg_ref[...]


def heads_of(q_ref, qs_ref):
    one = (lax.broadcasted_iota(jnp.int32, (T, HW), 1) == 0).astype(bf16)
    for h in range(QH):
        qs_ref[h * T : h * T + T, :HW] = q_ref[:, h * HW : (h + 1) * HW]
        qs_ref[h * T : h * T + T, HW:] = one


def fold(scores, values, m_ref, al_ref):
    s = scores(0)
    for h in range(QH):
        later = scores(h + 1) if h + 1 < QH else None
        m_old = m_ref[h]
        m_new = jnp.maximum(m_old, jnp.max(s, axis=1, keepdims=True))
        p = jnp.exp2(s * SCALE - tile_lanes(m_new * SCALE, s.shape[1] // 128)).astype(bf16)
        factor = jnp.exp2((m_old - m_new) * SCALE)
        al_ref[h] = al_ref[h] * tile_lanes(factor, 2) + nn(p, values)
        m_ref[h] = m_new
        s = later


def far_blocks(blocks, position, first, qs_ref, packs, m_ref, al_ref, k_ref, v_ref):
    n = len(blocks)
    touches, biases = False, []
    for which, base, behind in blocks:
        ids = packs[which][base + 2 * HW : base + ROWS, :].astype(f32)[:1, :]
        inside = position >= behind
        touches = touches | ((jnp.max(ids) == first) & inside)
        biases.append(jnp.where((ids == first) & inside, 0.0, LOW))

    @pl.when(touches)
    def _():
        top = lax.broadcasted_iota(jnp.int32, (16, T), 0) == 0
        for b, (which, base, _) in enumerate(blocks):
            ref = packs[which]
            c = slice(b * T, b * T + T)
            k_ref[:HW, c] = ref[base : base + HW, :]
            k_ref[HW : HW + 16, c] = jnp.where(top, biases[b], 0.0).astype(bf16)
            for i in range(3):
                row = b * T + i * 128
                v_ref[row : row + 128, :HW] = ref[base + HW : base + 2 * HW, i * 128 : i * 128 + 128]

        def scores(h):
            return nn(qs_ref[h * T : h * T + T, :], k_ref[:, : n * T])

        fold(scores, v_ref[: n * T, :], m_ref, al_ref)


def set_up(k_ref, v_ref):
    k_ref[HW:, :] = jnp.zeros((HW, k_ref.shape[1]), bf16)
    v_ref[:, HW:] = jnp.ones((v_ref.shape[0], HW), bf16)


def first_kernel(waves, n, q_hbm, own_ref, *refs):
    packs = refs[:n]
    m_ref, al_ref, q_ref, qs_ref, kt_ref, vs_ref, sems = refs[n:]
    copies = fetch([(q_hbm, q_ref)], sems)
    row = own_ref[2 * HW :, :].astype(f32)[:1, :]
    first, last = jnp.min(row), jnp.max(row)
    position = lax.axis_index("ctx")
    m_ref[...] = jnp.full(m_ref.shape, LOW, f32)
    al_ref[...] = jnp.zeros(al_ref.shape, f32)
    set_up(kt_ref, vs_ref)
    copies[0].wait()
    heads_of(q_ref, qs_ref)
    for blocks in waves:
        far_blocks(blocks, position, first, qs_ref, packs, m_ref, al_ref, kt_ref, vs_ref)
    own = column_of(row)

    @pl.when(last != first)
    def _():
        keeps = own == first

        @pl.loop(0, QH)
        def _(h):
            m_ref[h] = jnp.where(keeps, m_ref[h], LOW)
            al_ref[h] = jnp.where(tile_lanes(keeps, 2), al_ref[h], 0.0)

    order_t = lax.broadcasted_iota(jnp.int32, (T, T), 0)
    order_s = lax.broadcasted_iota(jnp.int32, (T, T), 1)
    allowed = (tile_lanes(own, 3) == row) & (order_s <= order_t)
    for c in range(3):
        vs_ref[c * 128 : c * 128 + 128, :HW] = own_ref[HW : 2 * HW, c * 128 : c * 128 + 128]

    def scores(h):
        return jnp.where(allowed, nn(qs_ref[h * T : h * T + T, :HW], own_ref[:HW, :]), LOW)

    fold(scores, vs_ref[:T, :], m_ref, al_ref)


def last_kernel(waves, n, q_hbm, wa_hbm, wm_hbm, normed_ref, doc_ref, m_in, al_in, *refs):
    packs = refs[:n]
    keep_ref, send_ref = refs[n : n + 2]
    m_ref, al_ref, q_ref, qs_ref, kt_ref, vs_ref, full_ref, both_ref, w_ref, sems = refs[n + 2 :]
    copies = fetch(
        [
            (q_hbm, q_ref),
            (wa_hbm, w_ref.at[: QH * HW]),
            (wm_hbm, w_ref.at[QH * HW :]),
        ],
        sems,
    )
    row = doc_ref[...].reshape(1, T).astype(f32)
    first, last = jnp.min(row), jnp.max(row)
    position = lax.axis_index("ctx")
    m_ref[...] = m_in[...]
    al_ref[...] = al_in[...]
    set_up(kt_ref, vs_ref)
    copies[0].wait()
    heads_of(q_ref, qs_ref)
    for blocks in waves:
        far_blocks(blocks, position, first, qs_ref, packs, m_ref, al_ref, kt_ref, vs_ref)

    @pl.when(last != first)
    def _():
        keeps = tile_lanes(column_of(row) == first, 2)

        @pl.loop(0, QH)
        def _(h):
            al_ref[h] = jnp.where(keeps, al_ref[h], al_in[h])

    for h in range(QH):
        full_ref[:, h * HW : (h + 1) * HW] = (
            al_ref[h, :, :HW] / al_ref[h, :, HW:]
        ).astype(bf16)
    deal_rows(full_ref, both_ref.at[:, : QH * HW])
    both_ref[:, QH * HW :] = normed_ref[...]
    for copy in copies[1:]:
        copy.wait()
    for j in range(0, D, COLS):
        c = slice(j, j + COLS)
        part = nn(both_ref[...], w_ref[:, c]).astype(bf16)
        keep_ref[:, c] = part[: T // 2]
        send_ref[:, c] = part[T // 2 :]


STATE = [sds((QH, T, 128), f32), sds((QH, T, 256), f32)]


def widest(waves):
    return max(len(blocks) for blocks in waves) * T


def attend_first(waves, q, pack, packs):
    n = len(packs)
    return pl.pallas_call(
        functools.partial(first_kernel, waves, n),
        out_shape=STATE,
        in_specs=[HBM] + [VMEM] * (n + 1),
        out_specs=[VMEM] * 2,
        scratch_shapes=[
            pltpu.VMEM((T, QH * HW), bf16),
            pltpu.VMEM((QH * T, 2 * HW), bf16),
            pltpu.VMEM((2 * HW, widest(waves)), bf16),
            pltpu.VMEM((widest(waves), 2 * HW), bf16),
            pltpu.SemaphoreType.DMA((1,)),
        ],
        compiler_params=params(60),
        cost_estimate=cost(*COSTS["attend_first"]),
        name="attend_first",
    )(q, pack, *packs)


def attend_last(waves, q, w_attn, w_mamba, normed, doc_row, state, packs):
    n = len(packs)
    half = sds((T // 2, D), bf16)
    depth = QH * HW + MHL * PS
    return pl.pallas_call(
        functools.partial(last_kernel, waves, n),
        out_shape=[half, half],
        in_specs=[HBM] * 3 + [VMEM] * (n + 4),
        out_specs=[VMEM] * 2,
        scratch_shapes=[
            pltpu.VMEM((QH, T, 128), f32),
            pltpu.VMEM((QH, T, 256), f32),
            pltpu.VMEM((T, QH * HW), bf16),
            pltpu.VMEM((QH * T, 2 * HW), bf16),
            pltpu.VMEM((2 * HW, widest(waves)), bf16),
            pltpu.VMEM((widest(waves), 2 * HW), bf16),
            pltpu.VMEM((T, QH * HW), bf16),
            pltpu.VMEM((T, depth), bf16),
            pltpu.VMEM((depth, D), bf16),
            pltpu.SemaphoreType.DMA((3,)),
        ],
        compiler_params=params(52),
        cost_estimate=cost(*COSTS["attend_last"]),
        name="attend_last",
    )(q, w_attn, w_mamba, normed, doc_row, *state, *packs)


def combine_kernel(keep_ref, got_ref, own_ref, far_a_ref, far_b_ref, up_ref, down_ref):
    total = keep_ref[...].astype(f32) + got_ref[...].astype(f32)
    own_ref[...] = total[:48]
    up_ref[...] = total[48:96].astype(bf16)
    far_a_ref[...] = total[96:144, : D // 2].astype(bf16)
    far_b_ref[...] = total[96:144, D // 2 :].astype(bf16)
    down_ref[...] = total[144:].astype(bf16)


def combine(keep, got):
    wide, half = sds((48, D), bf16), sds((48, D // 2), bf16)
    return pl.pallas_call(
        combine_kernel,
        out_shape=[sds((48, D), f32), half, half, wide, wide],
        in_specs=[VMEM] * 2,
        out_specs=[VMEM] * 5,
        compiler_params=params(8),
        cost_estimate=cost(*COSTS["combine"]),
        name="combine",
    )(keep, got)


def add_far_kernel(at, a_ref, b_ref, out_ref):
    out_ref[...] = a_ref[...]
    c = slice(at, at + D // 2)
    out_ref[:, c] = (a_ref[:, c].astype(f32) + b_ref[...].astype(f32)).astype(bf16)


def add_far(a, b, at):
    return pl.pallas_call(
        functools.partial(add_far_kernel, at),
        out_shape=sds((48, D), bf16),
        in_specs=[VMEM] * 2,
        out_specs=VMEM,
        compiler_params=params(8),
        cost_estimate=cost(*COSTS["combine"]),
        name="add_far",
    )(a, b)


def along(v, by):
    n = lax.axis_size("ctx")
    return lax.ppermute(v, "ctx", [(i, (i + by) % n) for i in range(n)])


def from_previous(v):
    n = lax.axis_size("ctx")
    return lax.ppermute(v, "ctx", [(i, i + 1) for i in range(n - 1)])


def along_y(v, by):
    return lax.ppermute(
        v, "tp", [(2 * y + c, 2 * ((y + by) % 4) + c) for y in range(4) for c in range(2)]
    )


def other_core(v):
    return lax.ppermute(v, "tp", [(i, i ^ 1) for i in range(8)])


def body(
    query, key, value, doc_ids, mamba_x, mamba_bc, gate_z, dt_raw, decay_rate,
    conv_x, conv_bc, skip_gain, norm_gain, attn_out_weight, mamba_out_weight,
):
    doc_row = doc_ids
    bc = mamba_bc.reshape(T, 2 * NS)

    end = T // 16 - 1
    tail = pl.pallas_call(
        tail_kernel,
        grid=(1,),
        out_shape=sds((16, 896), bf16),
        in_specs=[
            pl.BlockSpec((16, 512), lambda i: (end, 0)),
            pl.BlockSpec((16, 256), lambda i: (end, 0)),
            VMEM,
        ],
        out_specs=VMEM,
        compiler_params=params(12),
        cost_estimate=cost(*COSTS["tail"]),
        name="tail",
    )(mamba_x, bc, doc_row)
    tail = from_previous(tail)
    pack = pl.pallas_call(
        pack_kernel,
        out_shape=sds((ROWS, T), bf16),
        in_specs=[HBM, HBM, VMEM, ANY],
        out_specs=VMEM,
        scratch_shapes=[pltpu.VMEM((T, HW), bf16)] * 2 + [pltpu.SemaphoreType.DMA((2,))],
        compiler_params=params(12),
        cost_estimate=cost(*COSTS["pack"]),
        name="pack",
    )(key, value, doc_row, tail)
    g1 = along(pack, 1)
    g8 = along(pack, 8)
    g16 = along(pack, 16)

    xc, bcc, cs, msg = pl.pallas_call(
        local_kernel,
        out_shape=[
            sds((T, MHL * PS), bf16), sds((T, 2 * NS), bf16), sds((16, T), f32),
            sds((32, 32, NS), bf16),
        ],
        in_specs=[HBM] * 4 + [VMEM] * 4,
        out_specs=[VMEM] * 4,
        scratch_shapes=[
            pltpu.VMEM((T + 16, 768), f32),
            pltpu.VMEM((T + 16, 128), f32),
            pltpu.VMEM((T, MHL * PS), bf16),
            pltpu.VMEM((MHL, T), f32),
            pltpu.VMEM((KW, MHL * PS), f32),
            pltpu.VMEM((MHL,), f32),
            pltpu.SemaphoreType.DMA((4,)),
        ],
        compiler_params=params(12),
        cost_estimate=cost(*COSTS["local"]),
        name="local",
    )(mamba_x, dt_raw, conv_x, decay_rate, bc, tail, doc_row, conv_bc.reshape(KW, 2 * NS))

    up, down, msg = pl.pallas_call(
        join_kernel,
        out_shape=[sds((2 * ROWS, T), bf16)] * 2 + [sds((32, 32, NS), bf16)],
        in_specs=[VMEM] * 4,
        out_specs=[VMEM] * 3,
        compiler_params=params(12),
        cost_estimate=cost(*COSTS["join"]),
        name="join",
    )(g1, g8, g16, msg)

    msg = lax.all_to_all(msg.reshape(32 * 32, NS), "ctx", 0, 0, tiled=True)

    c29 = along(up, 1)
    c715 = along(down, -1)
    g17 = along(g16, 1)

    y = pl.pallas_call(
        intra_kernel,
        out_shape=sds((T, MHL * PS), f32),
        in_specs=[VMEM] * 5 + [ANY] * 3,
        out_specs=VMEM,
        scratch_shapes=[pltpu.VMEM((T, T), f32)],
        compiler_params=params(12),
        cost_estimate=cost(*COSTS["intra"]),
        name="intra",
    )(xc, bcc, cs, doc_row, skip_gain, c29, c715, g17)

    carried = pl.pallas_call(
        scan_kernel,
        out_shape=sds((32, 16, NS), bf16),
        in_specs=[VMEM, ANY],
        out_specs=VMEM,
        cost_estimate=cost(*COSTS["scan"]),
        compiler_params=params(8),
        name="scan",
    )(msg.reshape(32, 32, NS), y)
    carried = lax.all_to_all(carried.reshape(32 * 16, NS), "ctx", 0, 0, tiled=True)

    c310 = along(c29, 1)
    c614 = along(c715, -1)
    state = attend_first(
        [
            [(0, 0, 1), (1, 0, 8), (2, 0, 16), (3, 0, 2), (3, ROWS, 9), (4, 0, 7)],
            [(4, ROWS, 15), (5, 0, 17), (6, 0, 3), (6, ROWS, 10), (7, 0, 6), (7, ROWS, 14)],
        ],
        query, pack, [g1, g8, g16, c29, c715, g17, c310, c614],
    )
    c411 = along(c310, 1)
    c513 = along(c614, -1)
    g12 = along(c310[:ROWS], 9)

    normed = pl.pallas_call(
        gated_kernel,
        out_shape=sds((T, MHL * PS), bf16),
        in_specs=[HBM] + [VMEM] * 7 + [ANY],
        out_specs=VMEM,
        scratch_shapes=[
            pltpu.VMEM((T, MHL * PS), bf16),
            pltpu.VMEM((T, MHL * PS), f32),
            pltpu.VMEM((T, MHL * PS), bf16),
            pltpu.SemaphoreType.DMA((1,)),
        ],
        compiler_params=params(12),
        cost_estimate=cost(*COSTS["gated"]),
        name="gated",
    )(gate_z, y, carried, bcc, cs, doc_row, tail, norm_gain.reshape(1, MHL * PS), state[0])

    keep, send = attend_last(
        [[(0, 0, 4), (0, ROWS, 11), (1, 0, 5), (1, ROWS, 13), (2, 0, 12)]],
        query, attn_out_weight, mamba_out_weight, normed, doc_row, state, [c411, c513, g12],
    )
    own, far_a, far_b, up, down = combine(keep, other_core(send))
    up = along_y(add_far(up, along_y(far_a, 1), 0), 1)
    down = along_y(add_far(down, along_y(far_b, -1), D // 2), -1)
    return (own + up.astype(f32) + down.astype(f32)).astype(bf16)


def solution(mesh):
    return jax.shard_map(
        body,
        mesh=mesh,
        in_specs=(
            P("ctx", "tp"), P("ctx", "tp"), P("ctx", "tp"), P("ctx"), P("ctx", "tp"),
            P("ctx", None, "tp"), P("ctx", "tp"), P("tp", "ctx"), P("tp"), P(None, "tp"),
            P(None, None, "tp"), P("tp"), P("tp"), P("tp", None), P("tp", None),
        ),
        out_specs=P(("ctx", "tp"), None),
        check_vma=False,
    )
```

```python
import functools
import math

import jax
import jax.numpy as jnp
from jax import lax
from jax.experimental import pallas as pl
from jax.experimental.pallas import tpu as pltpu
from jax.sharding import PartitionSpec as P

T = 384
HW = 128
QH = 4
MHL = 8
PS = 64
NS = 128
KW = 4
D = 5120
COLS = 512
ROWS = 2 * HW + 16
LOW = -1e30
SCALE = HW**-0.5 * math.log2(math.e)
f32 = jnp.float32
bf16 = jnp.bfloat16

VMEM = pl.BlockSpec(memory_space=pltpu.VMEM)
ANY = pl.BlockSpec(memory_space=pl.ANY)
HBM = pl.BlockSpec(memory_space=pltpu.HBM)


def params(mib):
    return pltpu.CompilerParams(vmem_limit_bytes=mib * 2**20)


def cost(flops, nbytes, trans=0):
    return pl.CostEstimate(flops=int(flops), bytes_accessed=int(nbytes), transcendentals=int(trans))


COSTS = {
    "tail": (1e6, 1e4),
    "pack": (1e6, 1e4),
    "prepare": (1e6, 1e4),
    "local": (1e6, 1e4),
    "join": (1e6, 1e4),
    "tie": (1e6, 1e4),
    "intra": (5e10, 1e6),
    "scan": (1e6, 1e4),
    "attend_first": (5e10, 1e6),
    "attend_last": (1e6, 1e4),
    "combine": (1e6, 1e4),
}


def sds(shape, dtype):
    return jax.ShapeDtypeStruct(shape, dtype)


def nt(a, b):
    return lax.dot_general(a, b, (((1,), (1,)), ((), ())), preferred_element_type=f32)


def nn(a, b):
    return lax.dot_general(a, b, (((1,), (0,)), ((), ())), preferred_element_type=f32)


def column_of(row):
    return jnp.transpose(jnp.broadcast_to(row, (128, T)))


def columns_of(rows):
    return jnp.transpose(jnp.concatenate([rows, jnp.zeros((120, T), f32)], axis=0))


def column_of_eight(ref):
    row = jnp.broadcast_to(ref[...].reshape(1, 8), (8, 8))
    same = lax.broadcasted_iota(jnp.int32, (8, 8), 0) == lax.broadcasted_iota(jnp.int32, (8, 8), 1)
    return jnp.sum(jnp.where(same, row, 0.0), axis=1, keepdims=True)


def fetch(pairs, sems):
    copies = [pltpu.make_async_copy(a, b, sems.at[i]) for i, (a, b) in enumerate(pairs)]
    for copy in copies:
        copy.start()
    return copies


def tile_lanes(a, n):
    return jnp.concatenate([a] * n, axis=1)


def convolve(ext_ref, dex_ref, taps_ref, r, rows, xc_ref, bcc_ref):
    acc = [jnp.zeros((rows, 128), f32) for _ in range(6)]
    for k in range(KW):
        lo = r + 13 + k
        same = (dex_ref[lo : lo + rows, :] == dex_ref[r + 16 : r + 16 + rows, :]).astype(f32)
        for c in range(6):
            lanes = slice(c * 128, c * 128 + 128)
            acc[c] = acc[c] + taps_ref[k : k + 1, lanes] * ext_ref[lo : lo + rows, lanes] * same
    for c in range(6):
        v = jax.nn.silu(acc[c]).astype(bf16)
        if c < 4:
            xc_ref[r : r + rows, c * 128 : c * 128 + 128] = v
        else:
            bcc_ref[r : r + rows, (c - 4) * 128 : (c - 4) * 128 + 128] = v


def prepare_kernel(
    x_hbm, dt_hbm, cx_hbm, rate_hbm, bc_ref, doc_ref, cbc_ref,
    xc_ref, bcc_ref, cs_ref, taps_ref, head_ref,
    ext_ref, dex_ref, x_ref, dt_ref, cx_ref, rate_ref, sems,
):
    copies = fetch(
        [(x_hbm, x_ref), (dt_hbm, dt_ref), (cx_hbm, cx_ref), (rate_hbm, rate_ref)], sems
    )
    dex_ref[:16, :] = jnp.zeros((16, 128), f32)
    dex_ref[16:, :] = column_of(doc_ref[...].reshape(1, T).astype(f32) + 1.0)
    ext_ref[:16, :] = jnp.zeros((16, 768), f32)
    ext_ref[16:, 512:] = bc_ref[...].astype(f32)
    taps_ref[:, 512:] = cbc_ref[...]
    for copy in copies:
        copy.wait()
    taps_ref[:, :512] = cx_ref[...]
    ext_ref[16:, :512] = x_ref[...].astype(f32)
    head_ref[:, :768] = ext_ref[16:32, :]
    head_ref[:, 768:] = dex_ref[16:32, :]
    for r in range(0, T, 128):
        convolve(ext_ref, dex_ref, taps_ref, r, 128, xc_ref, bcc_ref)
    dt = dt_ref[...]
    step = jnp.maximum(dt, 0.0) + jnp.log1p(jnp.exp(-jnp.abs(dt)))
    rate = column_of_eight(rate_ref)
    tri = (
        lax.broadcasted_iota(jnp.int32, (T, T), 0) <= lax.broadcasted_iota(jnp.int32, (T, T), 1)
    ).astype(f32)
    cs_ref[:8, :] = lax.dot_general(
        -step * rate, tri, (((1,), (0,)), ((), ())),
        precision=lax.Precision.HIGHEST, preferred_element_type=f32,
    )
    cs_ref[8:, :] = step


def local_kernel(
    xp_ref, bcp_ref, csp_ref, taps_ref, head_ref, g1_ref, doc_ref,
    xc_ref, bcc_ref, cs_ref, msg_ref, ext_ref, dex_ref,
):
    tail = g1_ref[ROWS:, :].astype(f32)
    before = jnp.where(lax.axis_index("ctx") > 0, tail[32:48, :128], 0.0)
    ext_ref[:16, :T] = tail[:16]
    ext_ref[:16, T:] = tail[16:32]
    ext_ref[16:, :] = head_ref[:, :768]
    dex_ref[:16, :] = before
    dex_ref[16:, :] = head_ref[:, 768:]
    xc_ref[...] = xp_ref[...]
    bcc_ref[...] = bcp_ref[...]
    convolve(ext_ref, dex_ref, taps_ref, 0, 16, xc_ref, bcc_ref)
    cum, step = csp_ref[:8, :], csp_ref[8:, :]
    cs_ref[:16, :] = csp_ref[...]
    cs_ref[16:, :] = jnp.concatenate([before[8:16]] * 3, axis=1)

    row = doc_ref[...].reshape(1, T).astype(f32)
    first, last = jnp.min(row), jnp.max(row)
    cum_end = cum[:, T - 1 :]
    end_w = jnp.where(row == last, jnp.exp(cum_end - cum) * step, 0.0)
    xt = jnp.transpose(xc_ref[...].astype(f32))
    xw = (xt.reshape(MHL, PS, T) * end_w[:, None, :]).reshape(MHL * PS, T).astype(bf16)
    state = nn(xw, bcc_ref[:, :NS])
    msg_ref[:, :16, :] = state.astype(bf16).reshape(32, 16, NS)
    whole = jnp.logical_and(before[15:16] == first + 1.0, last == first).astype(f32)
    gain = jnp.exp(cum_end) * whole
    high = gain.astype(bf16).astype(f32)
    low = gain - high
    at = lax.broadcasted_iota(jnp.int32, (MHL, 16, NS), 1)
    block = jnp.where(
        at == 0, high[:, None, :], jnp.where(at == 1, low[:, None, :], 0.0)
    ).astype(bf16)
    for q in range(4):
        for h in range(MHL):
            msg_ref[h * 4 + q, 16:, :] = block[h]


def scan_kernel(msg_ref, _, out_ref):
    state = jnp.zeros((16, NS), f32)
    for j in range(32):
        out_ref[j] = state.astype(bf16)
        block = msg_ref[j].astype(f32)
        state = (block[16:17] + block[17:18]) * state + block[:16]


def intra_kernel(xc_ref, bcc_ref, cs_ref, doc_ref, skip_ref, *refs):
    y_ref, cb_ref = refs[-2:]
    skip = column_of_eight(skip_ref)
    row = doc_ref[...].reshape(1, T).astype(f32)
    own = column_of(row)
    order_t = lax.broadcasted_iota(jnp.int32, (T, T), 0)
    order_s = lax.broadcasted_iota(jnp.int32, (T, T), 1)
    allowed = (tile_lanes(own, 3) == row) & (order_s <= order_t)
    cb_ref[...] = jnp.where(allowed, nt(bcc_ref[:, NS:], bcc_ref[:, :NS]), 0.0)
    cum = cs_ref[:8, :]
    cum_t = columns_of(cum)
    late = cum - jnp.log(cs_ref[8:16, :])
    for r in range(0, T, 128):
        k = r + 128
        cb = cb_ref[r:k, :k]
        for pair in range(MHL // 2):
            halves = []
            for h in (2 * pair, 2 * pair + 1):
                gap = cum_t[r:k, h : h + 1] - late[h : h + 1, :k]
                mix = (jnp.exp(jnp.minimum(gap, 60.0)) * cb).astype(bf16)
                x = xc_ref[:k, h * PS : (h + 1) * PS]
                halves.append(nn(mix, x) + skip[h : h + 1] * x[r:k].astype(f32))
            y_ref[r:k, pair * 128 : pair * 128 + 128] = jnp.concatenate(halves, axis=1)


def deal_rows(full_ref, out_ref):
    tp = lax.axis_index("tp")
    core = lax.rem(tp, 2)
    for d, ahead in enumerate((2, 0, 1, 3)):
        base = 2 * lax.rem(tp // 2 + ahead, 4)
        mine = pl.multiple_of((base + core) * 48, 16)
        other = pl.multiple_of((base + 1 - core) * 48, 16)
        out_ref[d * 48 : d * 48 + 48, :] = full_ref[pl.ds(mine, 48), :]
        out_ref[192 + d * 48 : 240 + d * 48, :] = full_ref[pl.ds(other, 48), :]


def gated_norm(z_ref, y_ref, state_ref, bcc_ref, cs_ref, doc_ref, gain_ref, g_ref, full_ref):
    own = column_of(doc_ref[...].reshape(1, T).astype(f32) + 1.0)
    prev = cs_ref[23:24, :128]
    entry = jnp.exp(columns_of(cs_ref[:8, :])) * (own == prev).astype(f32)
    from_state = nt(bcc_ref[:, NS:], state_ref[...])
    lane = lax.broadcasted_iota(jnp.int32, (T, 128), 1)
    total = jnp.zeros((T, 1), f32)
    for pair in range(MHL // 2):
        c = slice(pair * 128, pair * 128 + 128)
        e = jnp.where(
            lane < PS, entry[:, 2 * pair : 2 * pair + 1], entry[:, 2 * pair + 1 : 2 * pair + 2]
        )
        g = (y_ref[:, c] + from_state[:, c] * e) * jax.nn.silu(z_ref[:, c].astype(f32))
        g_ref[:, c] = g
        total = total + jnp.sum(g * g, axis=1, keepdims=True)
    inverse = lax.rsqrt(total * (1.0 / (MHL * PS)) + 1e-05)
    full_ref[...] = (g_ref[...] * inverse * gain_ref[...]).astype(bf16)


def pack_kernel(k_hbm, v_hbm, x_ref, bc_ref, doc_ref, pack_ref, next_ref, k_ref, v_ref, sems):
    copies = fetch([(k_hbm, k_ref), (v_hbm, v_ref)], sems)
    row = doc_ref[...].reshape(1, T).astype(f32)
    ids = jnp.broadcast_to(row, (16, T)).astype(bf16)
    next_ref[ROWS : ROWS + 16, :] = x_ref[:, :T]
    next_ref[ROWS + 16 : ROWS + 32, :128] = x_ref[:, T:]
    next_ref[ROWS + 16 : ROWS + 32, 128:] = bc_ref[...]
    last_ids = (column_of(row)[T - 16 :] + 1.0).astype(bf16)
    next_ref[ROWS + 32 :, :] = jnp.concatenate([last_ids] * 3, axis=1)
    for copy in copies:
        copy.wait()
    keys = jnp.transpose(k_ref[...].astype(f32)).astype(bf16)
    for ref in (pack_ref, next_ref):
        ref[:HW, :] = keys
        for c in range(3):
            ref[HW : 2 * HW, c * 128 : c * 128 + 128] = v_ref[c * 128 : c * 128 + 128, :]
        ref[2 * HW : ROWS, :] = ids


def join_kernel(a_ref, b_ref, c_ref, msg_ref, up_ref, down_ref, out_ref):
    up_ref[:ROWS] = a_ref[:ROWS]
    up_ref[ROWS:] = b_ref[...]
    down_ref[:ROWS] = b_ref[...]
    down_ref[ROWS:] = c_ref[...]
    out_ref[...] = msg_ref[...]


def heads_of(q_ref, qs_ref):
    one = (lax.broadcasted_iota(jnp.int32, (T, HW), 1) == 0).astype(bf16)
    for h in range(QH):
        qs_ref[h * T : h * T + T, :HW] = q_ref[:, h * HW : (h + 1) * HW]
        qs_ref[h * T : h * T + T, HW:] = one


def fold(scores, values, m_ref, al_ref):
    s = scores(0)
    for h in range(QH):
        later = scores(h + 1) if h + 1 < QH else None
        m_old = m_ref[h]
        m_new = jnp.maximum(m_old, jnp.max(s, axis=1, keepdims=True))
        p = jnp.exp2(s * SCALE - tile_lanes(m_new * SCALE, s.shape[1] // 128)).astype(bf16)
        factor = jnp.exp2((m_old - m_new) * SCALE)
        al_ref[h] = al_ref[h] * tile_lanes(factor, 2) + nn(p, values)
        m_ref[h] = m_new
        s = later


def far_blocks(blocks, position, first, qs_ref, packs, m_ref, al_ref, k_ref, v_ref):
    n = len(blocks)
    touches, biases = False, []
    for which, base, behind in blocks:
        ids = packs[which][base + 2 * HW : base + ROWS, :].astype(f32)[:1, :]
        inside = position >= behind
        touches = touches | ((jnp.max(ids) == first) & inside)
        biases.append(jnp.where((ids == first) & inside, 0.0, LOW))

    @pl.when(touches)
    def _():
        top = lax.broadcasted_iota(jnp.int32, (16, T), 0) == 0
        for b, (which, base, _) in enumerate(blocks):
            ref = packs[which]
            c = slice(b * T, b * T + T)
            k_ref[:HW, c] = ref[base : base + HW, :]
            k_ref[HW : HW + 16, c] = jnp.where(top, biases[b], 0.0).astype(bf16)
            for i in range(3):
                row = b * T + i * 128
                v_ref[row : row + 128, :HW] = ref[base + HW : base + 2 * HW, i * 128 : i * 128 + 128]

        def scores(h):
            return nn(qs_ref[h * T : h * T + T, :], k_ref[:, : n * T])

        fold(scores, v_ref[: n * T, :], m_ref, al_ref)


def set_up(k_ref, v_ref):
    k_ref[HW:, :] = jnp.zeros((HW, k_ref.shape[1]), bf16)
    v_ref[:, HW:] = jnp.ones((v_ref.shape[0], HW), bf16)


def first_kernel(waves, n, q_hbm, own_ref, *refs):
    packs = refs[:n]
    m_ref, al_ref, q_ref, qs_ref, kt_ref, vs_ref, sems = refs[n:]
    copies = fetch([(q_hbm, q_ref)], sems)
    row = own_ref[2 * HW :, :].astype(f32)[:1, :]
    first, last = jnp.min(row), jnp.max(row)
    position = lax.axis_index("ctx")
    m_ref[...] = jnp.full(m_ref.shape, LOW, f32)
    al_ref[...] = jnp.zeros(al_ref.shape, f32)
    set_up(kt_ref, vs_ref)
    copies[0].wait()
    heads_of(q_ref, qs_ref)
    for blocks in waves:
        far_blocks(blocks, position, first, qs_ref, packs, m_ref, al_ref, kt_ref, vs_ref)
    own = column_of(row)

    @pl.when(last != first)
    def _():
        keeps = own == first

        @pl.loop(0, QH)
        def _(h):
            m_ref[h] = jnp.where(keeps, m_ref[h], LOW)
            al_ref[h] = jnp.where(tile_lanes(keeps, 2), al_ref[h], 0.0)

    order_t = lax.broadcasted_iota(jnp.int32, (T, T), 0)
    order_s = lax.broadcasted_iota(jnp.int32, (T, T), 1)
    allowed = (tile_lanes(own, 3) == row) & (order_s <= order_t)
    for c in range(3):
        vs_ref[c * 128 : c * 128 + 128, :HW] = own_ref[HW : 2 * HW, c * 128 : c * 128 + 128]

    def scores(h):
        return jnp.where(allowed, nn(qs_ref[h * T : h * T + T, :HW], own_ref[:HW, :]), LOW)

    fold(scores, vs_ref[:T, :], m_ref, al_ref)


def last_kernel(waves, n, doc_ref, gain_ref, *refs):
    packs = refs[:n]
    q_hbm, m_hbm, al_hbm, z_hbm, y_hbm, state_hbm, bcc_hbm, cs_hbm, wa_hbm, wm_hbm = refs[n : n + 10]
    outs = refs[n + 10 : n + 16]
    (
        m_ref, al_ref, q_ref, m_in, al_in, z_ref, y_ref, state_ref, bcc_ref, cs_ref, w_ref,
        qs_ref, kt_ref, vs_ref, full_ref, g_ref, both_ref, part_ref, sems, out_sems,
    ) = refs[n + 16 :]
    copies = fetch(
        [
            (q_hbm, q_ref),
            (m_hbm, m_in),
            (al_hbm, al_in),
            (z_hbm, z_ref),
            (y_hbm, y_ref),
            (state_hbm, state_ref),
            (bcc_hbm, bcc_ref),
            (cs_hbm, cs_ref),
            (wa_hbm, w_ref.at[: QH * HW]),
            (wm_hbm, w_ref.at[QH * HW :]),
        ],
        sems,
    )
    row = doc_ref[...].reshape(1, T).astype(f32)
    first, last = jnp.min(row), jnp.max(row)
    position = lax.axis_index("ctx")
    m_ref[...] = jnp.full(m_ref.shape, LOW, f32)
    al_ref[...] = jnp.zeros(al_ref.shape, f32)
    set_up(kt_ref, vs_ref)
    copies[0].wait()
    heads_of(q_ref, qs_ref)
    for blocks in waves:
        far_blocks(blocks, position, first, qs_ref, packs, m_ref, al_ref, kt_ref, vs_ref)

    for copy in copies[1:8]:
        copy.wait()
    gated_norm(z_ref, y_ref, state_ref, bcc_ref, cs_ref, doc_ref, gain_ref, g_ref, full_ref)
    deal_rows(full_ref, both_ref.at[:, QH * HW :])
    keeps = column_of(row) == first
    for h in range(QH):
        m_far = jnp.where(keeps, m_ref[h], LOW)
        m_old = m_in[h]
        m = jnp.maximum(m_far, m_old)
        far, old = jnp.exp2((m_far - m) * SCALE), jnp.exp2((m_old - m) * SCALE)
        far = jnp.where(keeps, far, 0.0)
        top = al_ref[h, :, :HW] * far + al_in[h, :, :HW] * old
        bottom = al_ref[h, :, HW:] * far + al_in[h, :, HW:] * old
        full_ref[:, h * HW : (h + 1) * HW] = (top / bottom).astype(bf16)
    deal_rows(full_ref, both_ref.at[:, : QH * HW])
    for copy in copies[8:]:
        copy.wait()
    sent = []
    for j in range(0, D, COLS):
        c = pl.ds(j, COLS)
        part_ref[:, c] = nn(both_ref[...], w_ref[:, c]).astype(bf16)
        sent += fetch(
            [
                (part_ref.at[:48, c], outs[0].at[:, c]),
                (part_ref.at[48:96, c], outs[1].at[:, c]),
                (part_ref.at[96:144, c], outs[2].at[:, c]),
                (part_ref.at[144:192, c], outs[3].at[:, c]),
                (part_ref.at[192:240, c], outs[4].at[:, c]),
                (part_ref.at[240:, c], outs[5].at[:, c]),
            ],
            out_sems.at[j // COLS],
        )
    for copy in sent:
        copy.wait()


STATE = [sds((QH, T, 128), f32), sds((QH, T, 256), f32)]


def widest(waves):
    return max(len(blocks) for blocks in waves) * T


def attend_first(waves, q, pack, packs):
    n = len(packs)
    return pl.pallas_call(
        functools.partial(first_kernel, waves, n),
        out_shape=STATE,
        in_specs=[HBM] + [VMEM] * (n + 1),
        out_specs=[VMEM] * 2,
        scratch_shapes=[
            pltpu.VMEM((T, QH * HW), bf16),
            pltpu.VMEM((QH * T, 2 * HW), bf16),
            pltpu.VMEM((2 * HW, widest(waves)), bf16),
            pltpu.VMEM((widest(waves), 2 * HW), bf16),
            pltpu.SemaphoreType.DMA((1,)),
        ],
        compiler_params=params(24),
        cost_estimate=cost(*COSTS["attend_first"]),
        name="attend_first",
    )(q, pack, *packs)


def attend_last(waves, doc_row, gain, packs, *arrays):
    n = len(packs)
    pieces = [sds((48, D), bf16)] * 5 + [sds((144, D), bf16)]
    depth = QH * HW + MHL * PS
    return pl.pallas_call(
        functools.partial(last_kernel, waves, n),
        out_shape=pieces,
        in_specs=[VMEM] * (n + 2) + [HBM] * 10,
        out_specs=[HBM] * 6,
        scratch_shapes=[
            pltpu.VMEM((QH, T, 128), f32),
            pltpu.VMEM((QH, T, 256), f32),
            *[pltpu.VMEM(a.shape, a.dtype) for a in arrays[:8]],
            pltpu.VMEM((depth, D), bf16),
            pltpu.VMEM((QH * T, 2 * HW), bf16),
            pltpu.VMEM((2 * HW, widest(waves)), bf16),
            pltpu.VMEM((widest(waves), 2 * HW), bf16),
            pltpu.VMEM((T, QH * HW), bf16),
            pltpu.VMEM((T, MHL * PS), f32),
            pltpu.VMEM((T, depth), bf16),
            pltpu.VMEM((T, D), bf16),
            pltpu.SemaphoreType.DMA((10,)),
            pltpu.SemaphoreType.DMA((D // COLS, 6)),
        ],
        compiler_params=params(58),
        cost_estimate=cost(*COSTS["attend_last"]),
        name="attend_last",
    )(doc_row, gain, *packs, *arrays)


def far_kernel(keep_ref, got_ref, a_ref, b_ref):
    total = keep_ref[...].astype(f32) + got_ref[...].astype(f32)
    a_ref[...] = total[:, : D // 2].astype(bf16)
    b_ref[...] = total[:, D // 2 :].astype(bf16)


def far_sum(keep, got):
    return pl.pallas_call(
        far_kernel,
        out_shape=[sds((48, D // 2), bf16)] * 2,
        in_specs=[VMEM] * 2,
        out_specs=[VMEM] * 2,
        compiler_params=params(8),
        cost_estimate=cost(*COSTS["combine"]),
        name="far_sum",
    )(keep, got)


def near_kernel(row, at, keep_ref, got_ref, far_ref, out_ref):
    total = keep_ref[...].astype(f32) + got_ref[row : row + 48].astype(f32)
    out_ref[...] = total.astype(bf16)
    c = slice(at, at + D // 2)
    out_ref[:, c] = (total[:, c] + far_ref[...].astype(f32)).astype(bf16)


def near_sum(keep, got, far, row, at):
    return pl.pallas_call(
        functools.partial(near_kernel, row, at),
        out_shape=sds((48, D), bf16),
        in_specs=[VMEM] * 3,
        out_specs=VMEM,
        compiler_params=params(8),
        cost_estimate=cost(*COSTS["combine"]),
        name="near_sum",
    )(keep, got, far)


def own_kernel(keep_ref, got_ref, out_ref):
    out_ref[...] = keep_ref[...].astype(f32) + got_ref[:48].astype(f32)


def own_sum(keep, got):
    return pl.pallas_call(
        own_kernel,
        out_shape=sds((48, D), f32),
        in_specs=[VMEM] * 2,
        out_specs=VMEM,
        compiler_params=params(8),
        cost_estimate=cost(*COSTS["combine"]),
        name="own_sum",
    )(keep, got)


def along(v, by):
    n = lax.axis_size("ctx")
    return lax.ppermute(v, "ctx", [(i, (i + by) % n) for i in range(n)])


def from_previous(v):
    n = lax.axis_size("ctx")
    return lax.ppermute(v, "ctx", [(i, i + 1) for i in range(n - 1)])


def along_y(v, by):
    return lax.ppermute(
        v, "tp", [(2 * y + c, 2 * ((y + by) % 4) + c) for y in range(4) for c in range(2)]
    )


def other_core(v):
    return lax.ppermute(v, "tp", [(i, i ^ 1) for i in range(8)])


def body(
    query, key, value, doc_ids, mamba_x, mamba_bc, gate_z, dt_raw, decay_rate,
    conv_x, conv_bc, skip_gain, norm_gain, attn_out_weight, mamba_out_weight,
):
    doc_row = doc_ids
    bc = mamba_bc.reshape(T, 2 * NS)

    end = T // 16 - 1

    pack, onward = pl.pallas_call(
        pack_kernel,
        grid=(1,),
        out_shape=[sds((ROWS, T), bf16), sds((ROWS + 48, T), bf16)],
        in_specs=[
            HBM,
            HBM,
            pl.BlockSpec((16, MHL * PS), lambda i: (end, 0)),
            pl.BlockSpec((16, 2 * NS), lambda i: (end, 0)),
            VMEM,
        ],
        out_specs=[VMEM] * 2,
        scratch_shapes=[pltpu.VMEM((T, HW), bf16)] * 2 + [pltpu.SemaphoreType.DMA((2,))],
        compiler_params=params(60),
        cost_estimate=cost(*COSTS["pack"]),
        name="pack",
    )(key, value, mamba_x, bc, doc_row)
    g1 = along(onward, 1)
    g8 = along(pack, 8)
    g16 = along(pack, 16)

    prepared = pl.pallas_call(
        prepare_kernel,
        out_shape=[
            sds((T, MHL * PS), bf16), sds((T, 2 * NS), bf16), sds((16, T), f32),
            sds((KW, 768), f32), sds((16, 896), f32),
        ],
        in_specs=[HBM] * 4 + [VMEM] * 3,
        out_specs=[VMEM] * 5,
        scratch_shapes=[
            pltpu.VMEM((T + 16, 768), f32),
            pltpu.VMEM((T + 16, 128), f32),
            pltpu.VMEM((T, MHL * PS), bf16),
            pltpu.VMEM((MHL, T), f32),
            pltpu.VMEM((KW, MHL * PS), f32),
            pltpu.VMEM((MHL,), f32),
            pltpu.SemaphoreType.DMA((4,)),
        ],
        compiler_params=params(12),
        cost_estimate=cost(*COSTS["prepare"]),
        name="prepare",
    )(mamba_x, dt_raw, conv_x, decay_rate, bc, doc_row, conv_bc.reshape(KW, 2 * NS))
    xc, bcc, cs, msg = pl.pallas_call(
        local_kernel,
        out_shape=[
            sds((T, MHL * PS), bf16), sds((T, 2 * NS), bf16), sds((24, T), f32),
            sds((32, 32, NS), bf16),
        ],
        in_specs=[VMEM] * 7,
        out_specs=[VMEM] * 4,
        scratch_shapes=[pltpu.VMEM((32, 768), f32), pltpu.VMEM((32, 128), f32)],
        compiler_params=params(12),
        cost_estimate=cost(*COSTS["local"]),
        name="local",
    )(*prepared, g1, doc_row)

    up, down, msg = pl.pallas_call(
        join_kernel,
        out_shape=[sds((2 * ROWS, T), bf16)] * 2 + [sds((32, 32, NS), bf16)],
        in_specs=[VMEM] * 4,
        out_specs=[VMEM] * 3,
        compiler_params=params(12),
        cost_estimate=cost(*COSTS["join"]),
        name="join",
    )(g1, g8, g16, msg)

    msg = lax.all_to_all(msg.reshape(32 * 32, NS), "ctx", 0, 0, tiled=True)

    c29 = along(up, 1)
    c715 = along(down, -1)
    g17 = along(g16, 1)

    y = pl.pallas_call(
        intra_kernel,
        out_shape=sds((T, MHL * PS), f32),
        in_specs=[VMEM] * 5 + [ANY] * 3,
        out_specs=VMEM,
        scratch_shapes=[pltpu.VMEM((T, T), f32)],
        compiler_params=params(12),
        cost_estimate=cost(*COSTS["intra"]),
        name="intra",
    )(xc, bcc, cs, doc_row, skip_gain, c29, c715, g17)

    carried = pl.pallas_call(
        scan_kernel,
        out_shape=sds((32, 16, NS), bf16),
        in_specs=[VMEM, ANY],
        out_specs=VMEM,
        cost_estimate=cost(*COSTS["scan"]),
        compiler_params=params(8),
        name="scan",
    )(msg.reshape(32, 32, NS), y)
    carried = lax.all_to_all(carried.reshape(32 * 16, NS), "ctx", 0, 0, tiled=True)

    c310 = along(c29, 1)
    c614 = along(c715, -1)
    state = attend_first(
        [
            [(0, 0, 1), (1, 0, 8), (2, 0, 16), (3, 0, 2), (3, ROWS, 9), (4, 0, 7)],
            [(4, ROWS, 15), (5, 0, 17), (6, 0, 3), (6, ROWS, 10), (7, 0, 6), (7, ROWS, 14)],
        ],
        query, pack, [g1, g8, g16, c29, c715, g17, c310, c614],
    )
    c411 = along(c310, 1)
    c513 = along(c614, -1)
    g12 = along(c310[:ROWS], 9)

    keep_far, keep_own, keep_up, keep_down, send_far, send = attend_last(
        [[(0, 0, 4), (0, ROWS, 11), (1, 0, 5), (1, ROWS, 13), (2, 0, 12)]],
        doc_row, norm_gain.reshape(1, MHL * PS), [c411, c513, g12],
        query, *state, gate_z, y, carried, bcc, cs, attn_out_weight, mamba_out_weight,
    )
    far_a, far_b = far_sum(keep_far, other_core(send_far))
    got = other_core(send)
    up = along_y(near_sum(keep_up, got, along_y(far_a, 1), 48, 0), 1)
    down = along_y(near_sum(keep_down, got, along_y(far_b, -1), 96, D // 2), -1)
    own = own_sum(keep_own, got)
    return (own + up.astype(f32) + down.astype(f32)).astype(bf16)


def solution(mesh):
    return jax.shard_map(
        body,
        mesh=mesh,
        in_specs=(
            P("ctx", "tp"), P("ctx", "tp"), P("ctx", "tp"), P("ctx"), P("ctx", "tp"),
            P("ctx", None, "tp"), P("ctx", "tp"), P("tp", "ctx"), P("tp"), P(None, "tp"),
            P(None, None, "tp"), P("tp"), P("tp"), P("tp", None), P("tp", None),
        ),
        out_specs=P(("ctx", "tp"), None),
        check_vma=False,
    )
```

```python
import functools
import math

import jax
import jax.numpy as jnp
from jax import lax
from jax.experimental import pallas as pl
from jax.experimental.pallas import tpu as pltpu
from jax.sharding import PartitionSpec as P

T = 384
HW = 128
QH = 4
MHL = 8
PS = 64
NS = 128
KW = 4
D = 5120
COLS = 512
ROWS = 2 * HW + 16
LOW = -1e30
SCALE = HW**-0.5 * math.log2(math.e)
f32 = jnp.float32
bf16 = jnp.bfloat16

VMEM = pl.BlockSpec(memory_space=pltpu.VMEM)
ANY = pl.BlockSpec(memory_space=pl.ANY)
HBM = pl.BlockSpec(memory_space=pltpu.HBM)


def params(mib):
    return pltpu.CompilerParams(vmem_limit_bytes=mib * 2**20)


def cost(flops, nbytes, trans=0):
    return pl.CostEstimate(flops=int(flops), bytes_accessed=int(nbytes), transcendentals=int(trans))


COSTS = {
    "tail": (1e6, 1e4),
    "pack": (1e6, 1e4),
    "prepare": (1e6, 1e4),
    "local": (1e6, 1e4),
    "join": (1e6, 1e4),
    "tie": (1e6, 1e4),
    "intra": (5e10, 1e6),
    "scan": (1e6, 1e4),
    "attend_first": (5e10, 1e6),
    "attend_last": (1e6, 1e4),
    "combine": (1e6, 1e4),
}


def sds(shape, dtype):
    return jax.ShapeDtypeStruct(shape, dtype)


def nt(a, b):
    return lax.dot_general(a, b, (((1,), (1,)), ((), ())), preferred_element_type=f32)


def nn(a, b):
    return lax.dot_general(a, b, (((1,), (0,)), ((), ())), preferred_element_type=f32)


def column_of(row):
    return jnp.transpose(jnp.broadcast_to(row, (128, T)))


def columns_of(rows):
    return jnp.transpose(jnp.concatenate([rows, jnp.zeros((120, T), f32)], axis=0))


def column_of_eight(ref):
    row = jnp.broadcast_to(ref[...].reshape(1, 8), (8, 8))
    same = lax.broadcasted_iota(jnp.int32, (8, 8), 0) == lax.broadcasted_iota(jnp.int32, (8, 8), 1)
    return jnp.sum(jnp.where(same, row, 0.0), axis=1, keepdims=True)


def fetch(pairs, sems):
    copies = [pltpu.make_async_copy(a, b, sems.at[i]) for i, (a, b) in enumerate(pairs)]
    for copy in copies:
        copy.start()
    return copies


def tile_lanes(a, n):
    return jnp.concatenate([a] * n, axis=1)


def convolve(ext_ref, dex_ref, taps_ref, r, rows, xc_ref, bcc_ref):
    acc = [jnp.zeros((rows, 128), f32) for _ in range(6)]
    for k in range(KW):
        lo = r + 13 + k
        same = (dex_ref[lo : lo + rows, :] == dex_ref[r + 16 : r + 16 + rows, :]).astype(f32)
        for c in range(6):
            lanes = slice(c * 128, c * 128 + 128)
            acc[c] = acc[c] + taps_ref[k : k + 1, lanes] * ext_ref[lo : lo + rows, lanes] * same
    for c in range(6):
        v = jax.nn.silu(acc[c]).astype(bf16)
        if c < 4:
            xc_ref[r : r + rows, c * 128 : c * 128 + 128] = v
        else:
            bcc_ref[r : r + rows, (c - 4) * 128 : (c - 4) * 128 + 128] = v


def prepare_kernel(
    x_hbm, dt_hbm, cx_hbm, rate_hbm, bc_ref, doc_ref, cbc_ref,
    xc_ref, bcc_ref, cs_ref, taps_ref, head_ref,
    ext_ref, dex_ref, x_ref, dt_ref, cx_ref, rate_ref, sems,
):
    copies = fetch(
        [(x_hbm, x_ref), (dt_hbm, dt_ref), (cx_hbm, cx_ref), (rate_hbm, rate_ref)], sems
    )
    dex_ref[:16, :] = jnp.zeros((16, 128), f32)
    dex_ref[16:, :] = column_of(doc_ref[...].reshape(1, T).astype(f32) + 1.0)
    ext_ref[:16, :] = jnp.zeros((16, 768), f32)
    ext_ref[16:, 512:] = bc_ref[...].astype(f32)
    taps_ref[:, 512:] = cbc_ref[...]
    for copy in copies:
        copy.wait()
    taps_ref[:, :512] = cx_ref[...]
    ext_ref[16:, :512] = x_ref[...].astype(f32)
    head_ref[:, :768] = ext_ref[16:32, :]
    head_ref[:, 768:] = dex_ref[16:32, :]
    for r in range(0, T, 128):
        convolve(ext_ref, dex_ref, taps_ref, r, 128, xc_ref, bcc_ref)
    dt = dt_ref[...]
    step = jnp.maximum(dt, 0.0) + jnp.log1p(jnp.exp(-jnp.abs(dt)))
    rate = column_of_eight(rate_ref)
    tri = (
        lax.broadcasted_iota(jnp.int32, (T, T), 0) <= lax.broadcasted_iota(jnp.int32, (T, T), 1)
    ).astype(f32)
    cs_ref[:8, :] = lax.dot_general(
        -step * rate, tri, (((1,), (0,)), ((), ())),
        precision=lax.Precision.HIGHEST, preferred_element_type=f32,
    )
    cs_ref[8:, :] = step


def local_kernel(
    xp_ref, bcp_ref, csp_ref, taps_ref, head_ref, g1_ref, doc_ref,
    xc_ref, bcc_ref, cs_ref, msg_ref, ext_ref, dex_ref,
):
    tail = g1_ref[ROWS:, :].astype(f32)
    before = jnp.where(lax.axis_index("ctx") > 0, tail[32:48, :128], 0.0)
    ext_ref[:16, :T] = tail[:16]
    ext_ref[:16, T:] = tail[16:32]
    ext_ref[16:, :] = head_ref[:, :768]
    dex_ref[:16, :] = before
    dex_ref[16:, :] = head_ref[:, 768:]
    xc_ref[...] = xp_ref[...]
    bcc_ref[...] = bcp_ref[...]
    convolve(ext_ref, dex_ref, taps_ref, 0, 16, xc_ref, bcc_ref)
    cum, step = csp_ref[:8, :], csp_ref[8:, :]
    cs_ref[:16, :] = csp_ref[...]
    cs_ref[16:, :] = jnp.concatenate([before[8:16]] * 3, axis=1)

    row = doc_ref[...].reshape(1, T).astype(f32)
    first, last = jnp.min(row), jnp.max(row)
    cum_end = cum[:, T - 1 :]
    end_w = jnp.where(row == last, jnp.exp(cum_end - cum) * step, 0.0)
    xt = jnp.transpose(xc_ref[...].astype(f32))
    xw = (xt.reshape(MHL, PS, T) * end_w[:, None, :]).reshape(MHL * PS, T).astype(bf16)
    state = nn(xw, bcc_ref[:, :NS])
    msg_ref[:, :16, :] = state.astype(bf16).reshape(32, 16, NS)
    whole = jnp.logical_and(before[15:16] == first + 1.0, last == first).astype(f32)
    gain = jnp.exp(cum_end) * whole
    high = gain.astype(bf16).astype(f32)
    low = gain - high
    at = lax.broadcasted_iota(jnp.int32, (MHL, 16, NS), 1)
    block = jnp.where(
        at == 0, high[:, None, :], jnp.where(at == 1, low[:, None, :], 0.0)
    ).astype(bf16)
    for q in range(4):
        for h in range(MHL):
            msg_ref[h * 4 + q, 16:, :] = block[h]


def scan_kernel(msg_ref, _, out_ref):
    state = jnp.zeros((16, NS), f32)
    for j in range(32):
        out_ref[j] = state.astype(bf16)
        block = msg_ref[j].astype(f32)
        state = (block[16:17] + block[17:18]) * state + block[:16]


def intra_kernel(xc_ref, bcc_ref, cs_ref, doc_ref, skip_ref, *refs):
    y_ref, cb_ref = refs[-2:]
    skip = column_of_eight(skip_ref)
    row = doc_ref[...].reshape(1, T).astype(f32)
    own = column_of(row)
    order_t = lax.broadcasted_iota(jnp.int32, (T, T), 0)
    order_s = lax.broadcasted_iota(jnp.int32, (T, T), 1)
    allowed = (tile_lanes(own, 3) == row) & (order_s <= order_t)
    cb_ref[...] = jnp.where(allowed, nt(bcc_ref[:, NS:], bcc_ref[:, :NS]), 0.0)
    cum = cs_ref[:8, :]
    cum_t = columns_of(cum)
    late = cum - jnp.log(cs_ref[8:16, :])
    for r in range(0, T, 128):
        k = r + 128
        cb = cb_ref[r:k, :k]
        for pair in range(MHL // 2):
            halves = []
            for h in (2 * pair, 2 * pair + 1):
                gap = cum_t[r:k, h : h + 1] - late[h : h + 1, :k]
                mix = (jnp.exp(jnp.minimum(gap, 60.0)) * cb).astype(bf16)
                x = xc_ref[:k, h * PS : (h + 1) * PS]
                halves.append(nn(mix, x) + skip[h : h + 1] * x[r:k].astype(f32))
            y_ref[r:k, pair * 128 : pair * 128 + 128] = jnp.concatenate(halves, axis=1)


def deal_rows(full_ref, out_ref):
    tp = lax.axis_index("tp")
    core = lax.rem(tp, 2)
    for d, ahead in enumerate((2, 0, 1, 3)):
        base = 2 * lax.rem(tp // 2 + ahead, 4)
        mine = pl.multiple_of((base + core) * 48, 16)
        other = pl.multiple_of((base + 1 - core) * 48, 16)
        out_ref[d * 48 : d * 48 + 48, :] = full_ref[pl.ds(mine, 48), :]
        out_ref[192 + d * 48 : 240 + d * 48, :] = full_ref[pl.ds(other, 48), :]


def gated_norm(z_ref, y_ref, state_ref, bcc_ref, cs_ref, doc_ref, gain_ref, g_ref, full_ref):
    own = column_of(doc_ref[...].reshape(1, T).astype(f32) + 1.0)
    prev = cs_ref[23:24, :128]
    entry = jnp.exp(columns_of(cs_ref[:8, :])) * (own == prev).astype(f32)
    from_state = nt(bcc_ref[:, NS:], state_ref[...])
    lane = lax.broadcasted_iota(jnp.int32, (T, 128), 1)
    total = jnp.zeros((T, 1), f32)
    for pair in range(MHL // 2):
        c = slice(pair * 128, pair * 128 + 128)
        e = jnp.where(
            lane < PS, entry[:, 2 * pair : 2 * pair + 1], entry[:, 2 * pair + 1 : 2 * pair + 2]
        )
        g = (y_ref[:, c] + from_state[:, c] * e) * jax.nn.silu(z_ref[:, c].astype(f32))
        g_ref[:, c] = g
        total = total + jnp.sum(g * g, axis=1, keepdims=True)
    inverse = lax.rsqrt(total * (1.0 / (MHL * PS)) + 1e-05)
    full_ref[...] = (g_ref[...] * inverse * gain_ref[...]).astype(bf16)


def pack_kernel(k_hbm, v_hbm, x_ref, bc_ref, doc_ref, pack_ref, next_ref, k_ref, v_ref, sems):
    copies = fetch([(k_hbm, k_ref), (v_hbm, v_ref)], sems)
    row = doc_ref[...].reshape(1, T).astype(f32)
    ids = jnp.broadcast_to(row, (16, T)).astype(bf16)
    next_ref[ROWS : ROWS + 16, :] = x_ref[:, :T]
    next_ref[ROWS + 16 : ROWS + 32, :128] = x_ref[:, T:]
    next_ref[ROWS + 16 : ROWS + 32, 128:] = bc_ref[...]
    last_ids = (column_of(row)[T - 16 :] + 1.0).astype(bf16)
    next_ref[ROWS + 32 :, :] = jnp.concatenate([last_ids] * 3, axis=1)
    for copy in copies:
        copy.wait()
    keys = jnp.transpose(k_ref[...].astype(f32)).astype(bf16)
    for ref in (pack_ref, next_ref):
        ref[:HW, :] = keys
        for c in range(3):
            ref[HW : 2 * HW, c * 128 : c * 128 + 128] = v_ref[c * 128 : c * 128 + 128, :]
        ref[2 * HW : ROWS, :] = ids


def join_kernel(a_ref, b_ref, c_ref, msg_ref, up_ref, down_ref, out_ref):
    up_ref[:ROWS] = a_ref[:ROWS]
    up_ref[ROWS:] = b_ref[...]
    down_ref[:ROWS] = b_ref[...]
    down_ref[ROWS:] = c_ref[...]
    out_ref[...] = msg_ref[...]


def heads_of(q_ref, qs_ref):
    one = (lax.broadcasted_iota(jnp.int32, (T, HW), 1) == 0).astype(bf16)
    for h in range(QH):
        qs_ref[h * T : h * T + T, :HW] = q_ref[:, h * HW : (h + 1) * HW]
        qs_ref[h * T : h * T + T, HW:] = one


def fold(scores, values, m_ref, al_ref):
    s = scores(0)
    for h in range(QH):
        later = scores(h + 1) if h + 1 < QH else None
        m_old = m_ref[h]
        m_new = jnp.maximum(m_old, jnp.max(s, axis=1, keepdims=True))
        p = jnp.exp2(s * SCALE - tile_lanes(m_new * SCALE, s.shape[1] // 128)).astype(bf16)
        factor = jnp.exp2((m_old - m_new) * SCALE)
        al_ref[h] = al_ref[h] * tile_lanes(factor, 2) + nn(p, values)
        m_ref[h] = m_new
        s = later


def far_blocks(blocks, position, first, qs_ref, packs, m_ref, al_ref, k_ref, v_ref):
    n = len(blocks)
    touches, biases = False, []
    for which, base, behind in blocks:
        ids = packs[which][base + 2 * HW : base + ROWS, :].astype(f32)[:1, :]
        inside = position >= behind
        touches = touches | ((jnp.max(ids) == first) & inside)
        biases.append(jnp.where((ids == first) & inside, 0.0, LOW))

    @pl.when(touches)
    def _():
        top = lax.broadcasted_iota(jnp.int32, (16, T), 0) == 0
        for b, (which, base, _) in enumerate(blocks):
            ref = packs[which]
            c = slice(b * T, b * T + T)
            k_ref[:HW, c] = ref[base : base + HW, :]
            k_ref[HW : HW + 16, c] = jnp.where(top, biases[b], 0.0).astype(bf16)
            for i in range(3):
                row = b * T + i * 128
                v_ref[row : row + 128, :HW] = ref[base + HW : base + 2 * HW, i * 128 : i * 128 + 128]

        def scores(h):
            return nn(qs_ref[h * T : h * T + T, :], k_ref[:, : n * T])

        fold(scores, v_ref[: n * T, :], m_ref, al_ref)


def set_up(k_ref, v_ref):
    k_ref[HW:, :] = jnp.zeros((HW, k_ref.shape[1]), bf16)
    v_ref[:, HW:] = jnp.ones((v_ref.shape[0], HW), bf16)


def first_kernel(waves, n, q_hbm, own_ref, *refs):
    packs = refs[:n]
    out_ref, m_ref, al_ref, q_ref, qs_ref, kt_ref, vs_ref, sems = refs[n:]
    copies = fetch([(q_hbm, q_ref)], sems)
    row = own_ref[2 * HW :, :].astype(f32)[:1, :]
    first, last = jnp.min(row), jnp.max(row)
    position = lax.axis_index("ctx")
    m_ref[...] = jnp.full(m_ref.shape, LOW, f32)
    al_ref[...] = jnp.zeros(al_ref.shape, f32)
    set_up(kt_ref, vs_ref)
    copies[0].wait()
    heads_of(q_ref, qs_ref)
    for blocks in waves:
        far_blocks(blocks, position, first, qs_ref, packs, m_ref, al_ref, kt_ref, vs_ref)
    own = column_of(row)

    @pl.when(last != first)
    def _():
        keeps = own == first

        @pl.loop(0, QH)
        def _(h):
            m_ref[h] = jnp.where(keeps, m_ref[h], LOW)
            al_ref[h] = jnp.where(tile_lanes(keeps, 2), al_ref[h], 0.0)

    order_t = lax.broadcasted_iota(jnp.int32, (T, T), 0)
    order_s = lax.broadcasted_iota(jnp.int32, (T, T), 1)
    allowed = (tile_lanes(own, 3) == row) & (order_s <= order_t)
    for c in range(3):
        vs_ref[c * 128 : c * 128 + 128, :HW] = own_ref[HW : 2 * HW, c * 128 : c * 128 + 128]

    def scores(h):
        return jnp.where(allowed, nn(qs_ref[h * T : h * T + T, :HW], own_ref[:HW, :]), LOW)

    fold(scores, vs_ref[:T, :], m_ref, al_ref)
    half = lax.broadcasted_iota(jnp.int32, (T, 128), 1) < 64
    for h in range(QH):
        out_ref[h, :, :HW] = al_ref[h, :, :HW]
        out_ref[h, :, HW:] = jnp.where(half, al_ref[h, :, HW:], m_ref[h])


def last_kernel(waves, n, doc_ref, gain_ref, *refs):
    packs = refs[:n]
    q_hbm, al_hbm, z_hbm, y_hbm, state_hbm, bcc_hbm, cs_hbm, wa_hbm, wm_hbm = refs[n : n + 9]
    outs = refs[n + 9 : n + 15]
    (
        m_ref, al_ref, q_ref, al_in, z_ref, y_ref, state_ref, bcc_ref, cs_ref, w_ref,
        qs_ref, kt_ref, vs_ref, full_ref, g_ref, both_ref, part_ref, sems, out_sems,
    ) = refs[n + 15 :]
    copies = fetch(
        [
            (q_hbm, q_ref),
            (al_hbm, al_in),
            (z_hbm, z_ref),
            (y_hbm, y_ref),
            (state_hbm, state_ref),
            (bcc_hbm, bcc_ref),
            (cs_hbm, cs_ref),
            (wa_hbm, w_ref.at[: QH * HW]),
            (wm_hbm, w_ref.at[QH * HW :]),
        ],
        sems,
    )
    row = doc_ref[...].reshape(1, T).astype(f32)
    first, last = jnp.min(row), jnp.max(row)
    position = lax.axis_index("ctx")
    m_ref[...] = jnp.full(m_ref.shape, LOW, f32)
    al_ref[...] = jnp.zeros(al_ref.shape, f32)
    set_up(kt_ref, vs_ref)
    copies[0].wait()
    heads_of(q_ref, qs_ref)
    for blocks in waves:
        far_blocks(blocks, position, first, qs_ref, packs, m_ref, al_ref, kt_ref, vs_ref)

    for copy in copies[1:7]:
        copy.wait()
    gated_norm(z_ref, y_ref, state_ref, bcc_ref, cs_ref, doc_ref, gain_ref, g_ref, full_ref)
    deal_rows(full_ref, both_ref.at[:, QH * HW :])
    keeps = column_of(row) == first
    for h in range(QH):
        m_far = jnp.where(keeps, m_ref[h], LOW)
        m_old = jnp.broadcast_to(al_in[h, :, 192:193], (T, 128))
        m = jnp.maximum(m_far, m_old)
        far, old = jnp.exp2((m_far - m) * SCALE), jnp.exp2((m_old - m) * SCALE)
        far = jnp.where(keeps, far, 0.0)
        top = al_ref[h, :, :HW] * far + al_in[h, :, :HW] * old
        bottom = al_ref[h, :, HW:] * far + jnp.broadcast_to(al_in[h, :, HW : HW + 1], (T, 128)) * old
        full_ref[:, h * HW : (h + 1) * HW] = (top / bottom).astype(bf16)
    deal_rows(full_ref, both_ref.at[:, : QH * HW])
    for copy in copies[7:]:
        copy.wait()
    sent = []
    for j in range(0, D, COLS):
        c = pl.ds(j, COLS)
        part_ref[:, c] = nn(both_ref[...], w_ref[:, c]).astype(bf16)
        sent += fetch(
            [
                (part_ref.at[:48, c], outs[0].at[:, c]),
                (part_ref.at[48:96, c], outs[1].at[:, c]),
                (part_ref.at[96:144, c], outs[2].at[:, c]),
                (part_ref.at[144:192, c], outs[3].at[:, c]),
                (part_ref.at[192:240, c], outs[4].at[:, c]),
                (part_ref.at[240:, c], outs[5].at[:, c]),
            ],
            out_sems.at[j // COLS],
        )
    for copy in sent:
        copy.wait()


STATE = sds((QH, T, 256), f32)


def widest(waves):
    return max(len(blocks) for blocks in waves) * T


def attend_first(waves, q, pack, packs):
    n = len(packs)
    return pl.pallas_call(
        functools.partial(first_kernel, waves, n),
        out_shape=STATE,
        in_specs=[HBM] + [VMEM] * (n + 1),
        out_specs=VMEM,
        scratch_shapes=[
            pltpu.VMEM((QH, T, 128), f32),
            pltpu.VMEM((QH, T, 256), f32),
            pltpu.VMEM((T, QH * HW), bf16),
            pltpu.VMEM((QH * T, 2 * HW), bf16),
            pltpu.VMEM((2 * HW, widest(waves)), bf16),
            pltpu.VMEM((widest(waves), 2 * HW), bf16),
            pltpu.SemaphoreType.DMA((1,)),
        ],
        compiler_params=params(60),
        cost_estimate=cost(*COSTS["attend_first"]),
        name="attend_first",
    )(q, pack, *packs)


def attend_last(waves, doc_row, gain, packs, *arrays):
    n = len(packs)
    pieces = [sds((48, D), bf16)] * 5 + [sds((144, D), bf16)]
    depth = QH * HW + MHL * PS
    return pl.pallas_call(
        functools.partial(last_kernel, waves, n),
        out_shape=pieces,
        in_specs=[VMEM] * (n + 2) + [HBM] * 9,
        out_specs=[HBM] * 6,
        scratch_shapes=[
            pltpu.VMEM((QH, T, 128), f32),
            pltpu.VMEM((QH, T, 256), f32),
            *[pltpu.VMEM(a.shape, a.dtype) for a in arrays[:7]],
            pltpu.VMEM((depth, D), bf16),
            pltpu.VMEM((QH * T, 2 * HW), bf16),
            pltpu.VMEM((2 * HW, widest(waves)), bf16),
            pltpu.VMEM((widest(waves), 2 * HW), bf16),
            pltpu.VMEM((T, QH * HW), bf16),
            pltpu.VMEM((T, MHL * PS), f32),
            pltpu.VMEM((T, depth), bf16),
            pltpu.VMEM((T, D), bf16),
            pltpu.SemaphoreType.DMA((9,)),
            pltpu.SemaphoreType.DMA((D // COLS, 6)),
        ],
        compiler_params=params(58),
        cost_estimate=cost(*COSTS["attend_last"]),
        name="attend_last",
    )(doc_row, gain, *packs, *arrays)


SPLIT = 2816


def far_kernel(keep_ref, got_ref, a_ref, b_ref):
    total = keep_ref[...].astype(f32) + got_ref[...].astype(f32)
    a_ref[...] = total[:, :SPLIT].astype(bf16)
    b_ref[...] = total[:, SPLIT:].astype(bf16)


def far_sum(keep, got):
    return pl.pallas_call(
        far_kernel,
        out_shape=[sds((48, SPLIT), bf16), sds((48, D - SPLIT), bf16)],
        in_specs=[VMEM] * 2,
        out_specs=[VMEM] * 2,
        compiler_params=params(8),
        cost_estimate=cost(*COSTS["combine"]),
        name="far_sum",
    )(keep, got)


def cores_kernel(own_ref, up_ref, down_ref, got_ref, *outs):
    for i, ref in enumerate((own_ref, up_ref, down_ref)):
        outs[i][...] = ref[...].astype(f32) + got_ref[48 * i : 48 * i + 48].astype(f32)


def cores_sum(own, up, down, got):
    return pl.pallas_call(
        cores_kernel,
        out_shape=[sds((48, D), f32)] * 3,
        in_specs=[VMEM] * 4,
        out_specs=[VMEM] * 3,
        compiler_params=params(8),
        cost_estimate=cost(*COSTS["combine"]),
        name="cores_sum",
    )(own, up, down, got)


def near_kernel(at, near_ref, far_ref, out_ref):
    out_ref[...] = near_ref[...].astype(bf16)
    c = slice(at, at + far_ref.shape[1])
    out_ref[:, c] = (near_ref[:, c] + far_ref[...].astype(f32)).astype(bf16)


def near_sum(near, far, at):
    return pl.pallas_call(
        functools.partial(near_kernel, at),
        out_shape=sds((48, D), bf16),
        in_specs=[VMEM] * 2,
        out_specs=VMEM,
        compiler_params=params(8),
        cost_estimate=cost(*COSTS["combine"]),
        name="near_sum",
    )(near, far)


def along(v, by):
    n = lax.axis_size("ctx")
    return lax.ppermute(v, "ctx", [(i, (i + by) % n) for i in range(n)])


def from_previous(v):
    n = lax.axis_size("ctx")
    return lax.ppermute(v, "ctx", [(i, i + 1) for i in range(n - 1)])


def along_y(v, by):
    return lax.ppermute(
        v, "tp", [(2 * y + c, 2 * ((y + by) % 4) + c) for y in range(4) for c in range(2)]
    )


def other_core(v):
    return lax.ppermute(v, "tp", [(i, i ^ 1) for i in range(8)])


def body(
    query, key, value, doc_ids, mamba_x, mamba_bc, gate_z, dt_raw, decay_rate,
    conv_x, conv_bc, skip_gain, norm_gain, attn_out_weight, mamba_out_weight,
):
    doc_row = doc_ids
    bc = mamba_bc.reshape(T, 2 * NS)

    end = T // 16 - 1

    pack, onward = pl.pallas_call(
        pack_kernel,
        grid=(1,),
        out_shape=[sds((ROWS, T), bf16), sds((ROWS + 48, T), bf16)],
        in_specs=[
            HBM,
            HBM,
            pl.BlockSpec((16, MHL * PS), lambda i: (end, 0)),
            pl.BlockSpec((16, 2 * NS), lambda i: (end, 0)),
            VMEM,
        ],
        out_specs=[VMEM] * 2,
        scratch_shapes=[pltpu.VMEM((T, HW), bf16)] * 2 + [pltpu.SemaphoreType.DMA((2,))],
        compiler_params=params(60),
        cost_estimate=cost(*COSTS["pack"]),
        name="pack",
    )(key, value, mamba_x, bc, doc_row)
    g1 = along(onward, 1)
    g8 = along(pack, 8)
    g16 = along(pack, 16)

    prepared = pl.pallas_call(
        prepare_kernel,
        out_shape=[
            sds((T, MHL * PS), bf16), sds((T, 2 * NS), bf16), sds((16, T), f32),
            sds((KW, 768), f32), sds((16, 896), f32),
        ],
        in_specs=[HBM] * 4 + [VMEM] * 3,
        out_specs=[VMEM] * 5,
        scratch_shapes=[
            pltpu.VMEM((T + 16, 768), f32),
            pltpu.VMEM((T + 16, 128), f32),
            pltpu.VMEM((T, MHL * PS), bf16),
            pltpu.VMEM((MHL, T), f32),
            pltpu.VMEM((KW, MHL * PS), f32),
            pltpu.VMEM((MHL,), f32),
            pltpu.SemaphoreType.DMA((4,)),
        ],
        compiler_params=params(12),
        cost_estimate=cost(*COSTS["prepare"]),
        name="prepare",
    )(mamba_x, dt_raw, conv_x, decay_rate, bc, doc_row, conv_bc.reshape(KW, 2 * NS))
    xc, bcc, cs, msg = pl.pallas_call(
        local_kernel,
        out_shape=[
            sds((T, MHL * PS), bf16), sds((T, 2 * NS), bf16), sds((24, T), f32),
            sds((32, 32, NS), bf16),
        ],
        in_specs=[VMEM] * 7,
        out_specs=[VMEM] * 4,
        scratch_shapes=[pltpu.VMEM((32, 768), f32), pltpu.VMEM((32, 128), f32)],
        compiler_params=params(12),
        cost_estimate=cost(*COSTS["local"]),
        name="local",
    )(*prepared, g1, doc_row)

    up, down, msg = pl.pallas_call(
        join_kernel,
        out_shape=[sds((2 * ROWS, T), bf16)] * 2 + [sds((32, 32, NS), bf16)],
        in_specs=[VMEM] * 4,
        out_specs=[VMEM] * 3,
        compiler_params=params(12),
        cost_estimate=cost(*COSTS["join"]),
        name="join",
    )(g1, g8, g16, msg)

    msg = lax.all_to_all(msg.reshape(32 * 32, NS), "ctx", 0, 0, tiled=True)

    c29 = along(up, 1)
    c715 = along(down, -1)
    g17 = along(g16, 1)

    y = pl.pallas_call(
        intra_kernel,
        out_shape=sds((T, MHL * PS), f32),
        in_specs=[VMEM] * 5 + [ANY] * 3,
        out_specs=VMEM,
        scratch_shapes=[pltpu.VMEM((T, T), f32)],
        compiler_params=params(12),
        cost_estimate=cost(*COSTS["intra"]),
        name="intra",
    )(xc, bcc, cs, doc_row, skip_gain, c29, c715, g17)

    carried = pl.pallas_call(
        scan_kernel,
        out_shape=sds((32, 16, NS), bf16),
        in_specs=[VMEM, ANY],
        out_specs=VMEM,
        cost_estimate=cost(*COSTS["scan"]),
        compiler_params=params(8),
        name="scan",
    )(msg.reshape(32, 32, NS), y)
    carried = lax.all_to_all(carried.reshape(32 * 16, NS), "ctx", 0, 0, tiled=True)

    c310 = along(c29, 1)
    c614 = along(c715, -1)
    state = attend_first(
        [
            [(0, 0, 1), (1, 0, 8), (2, 0, 16), (3, 0, 2), (3, ROWS, 9), (4, 0, 7)],
            [(4, ROWS, 15), (5, 0, 17), (6, 0, 3), (6, ROWS, 10), (7, 0, 6), (7, ROWS, 14)],
        ],
        query, pack, [g1, g8, g16, c29, c715, g17, c310, c614],
    )
    c411 = along(c310, 1)
    c513 = along(c614, -1)
    g12 = along(c310[:ROWS], 9)

    keep_far, keep_own, keep_up, keep_down, send_far, send = attend_last(
        [[(0, 0, 4), (0, ROWS, 11), (1, 0, 5), (1, ROWS, 13), (2, 0, 12)]],
        doc_row, norm_gain.reshape(1, MHL * PS), [c411, c513, g12],
        query, state, gate_z, y, carried, bcc, cs, attn_out_weight, mamba_out_weight,
    )
    far_a, far_b = far_sum(keep_far, other_core(send_far))
    own, up, down = cores_sum(keep_own, keep_up, keep_down, other_core(send))
    up = along_y(near_sum(up, along_y(far_a, 1), 0), 1)
    down = along_y(near_sum(down, along_y(far_b, -1), SPLIT), -1)
    return (own + up.astype(f32) + down.astype(f32)).astype(bf16)


def solution(mesh):
    return jax.shard_map(
        body,
        mesh=mesh,
        in_specs=(
            P("ctx", "tp"), P("ctx", "tp"), P("ctx", "tp"), P("ctx"), P("ctx", "tp"),
            P("ctx", None, "tp"), P("ctx", "tp"), P("tp", "ctx"), P("tp"), P(None, "tp"),
            P(None, None, "tp"), P("tp"), P("tp"), P("tp", None), P("tp", None),
        ),
        out_specs=P(("ctx", "tp"), None),
        check_vma=False,
    )
```

```python
import functools
import math

import jax
import jax.numpy as jnp
from jax import lax
from jax.experimental import pallas as pl
from jax.experimental.pallas import tpu as pltpu
from jax.sharding import PartitionSpec as P

T = 384
HW = 128
QH = 4
MHL = 8
PS = 64
NS = 128
KW = 4
D = 5120
COLS = 512
ROWS = 2 * HW + 16
LOW = -1e30
SCALE = HW**-0.5 * math.log2(math.e)
f32 = jnp.float32
bf16 = jnp.bfloat16

VMEM = pl.BlockSpec(memory_space=pltpu.VMEM)
ANY = pl.BlockSpec(memory_space=pl.ANY)
HBM = pl.BlockSpec(memory_space=pltpu.HBM)


def params(mib):
    return pltpu.CompilerParams(vmem_limit_bytes=mib * 2**20)


def cost(flops, nbytes, trans=0):
    return pl.CostEstimate(flops=int(flops), bytes_accessed=int(nbytes), transcendentals=int(trans))


COSTS = {
    "tail": (1e6, 1e4),
    "pack": (1e6, 1e4),
    "prepare": (1e6, 1e4),
    "local": (1e6, 1e4),
    "join": (1e6, 1e4),
    "tie": (1e6, 1e4),
    "intra": (5e10, 1e6),
    "scan": (1e6, 1e4),
    "attend_first": (5e10, 1e6),
    "attend_last": (1e6, 1e4),
    "combine": (1e6, 1e4),
}


def sds(shape, dtype):
    return jax.ShapeDtypeStruct(shape, dtype)


def nt(a, b):
    return lax.dot_general(a, b, (((1,), (1,)), ((), ())), preferred_element_type=f32)


def nn(a, b):
    return lax.dot_general(a, b, (((1,), (0,)), ((), ())), preferred_element_type=f32)


def column_of(row):
    return jnp.transpose(jnp.broadcast_to(row, (128, T)))


def columns_of(rows):
    return jnp.transpose(jnp.concatenate([rows, jnp.zeros((120, T), f32)], axis=0))


def column_of_eight(ref):
    row = jnp.broadcast_to(ref[...].reshape(1, 8), (8, 8))
    same = lax.broadcasted_iota(jnp.int32, (8, 8), 0) == lax.broadcasted_iota(jnp.int32, (8, 8), 1)
    return jnp.sum(jnp.where(same, row, 0.0), axis=1, keepdims=True)


def fetch(pairs, sems):
    copies = [pltpu.make_async_copy(a, b, sems.at[i]) for i, (a, b) in enumerate(pairs)]
    for copy in copies:
        copy.start()
    return copies


def tile_lanes(a, n):
    return jnp.concatenate([a] * n, axis=1)


def convolve(ext_ref, dex_ref, taps_ref, r, rows, xc_ref, bcc_ref):
    acc = [jnp.zeros((rows, 128), f32) for _ in range(6)]
    for k in range(KW):
        lo = r + 13 + k
        same = (dex_ref[lo : lo + rows, :] == dex_ref[r + 16 : r + 16 + rows, :]).astype(f32)
        for c in range(6):
            lanes = slice(c * 128, c * 128 + 128)
            acc[c] = acc[c] + taps_ref[k : k + 1, lanes] * ext_ref[lo : lo + rows, lanes] * same
    for c in range(6):
        v = jax.nn.silu(acc[c]).astype(bf16)
        if c < 4:
            xc_ref[r : r + rows, c * 128 : c * 128 + 128] = v
        else:
            bcc_ref[r : r + rows, (c - 4) * 128 : (c - 4) * 128 + 128] = v


def prepare_kernel(
    x_hbm, dt_hbm, cx_hbm, rate_hbm, bc_ref, doc_ref, cbc_ref,
    xc_ref, bcc_ref, cs_ref, taps_ref, head_ref,
    ext_ref, dex_ref, x_ref, dt_ref, cx_ref, rate_ref, sems,
):
    copies = fetch(
        [(x_hbm, x_ref), (dt_hbm, dt_ref), (cx_hbm, cx_ref), (rate_hbm, rate_ref)], sems
    )
    dex_ref[:16, :] = jnp.zeros((16, 128), f32)
    dex_ref[16:, :] = column_of(doc_ref[...].reshape(1, T).astype(f32) + 1.0)
    ext_ref[:16, :] = jnp.zeros((16, 768), f32)
    ext_ref[16:, 512:] = bc_ref[...].astype(f32)
    taps_ref[:, 512:] = cbc_ref[...]
    for copy in copies:
        copy.wait()
    taps_ref[:, :512] = cx_ref[...]
    ext_ref[16:, :512] = x_ref[...].astype(f32)
    head_ref[:, :768] = ext_ref[16:32, :]
    head_ref[:, 768:] = dex_ref[16:32, :]
    for r in range(0, T, 128):
        convolve(ext_ref, dex_ref, taps_ref, r, 128, xc_ref, bcc_ref)
    dt = dt_ref[...]
    step = jnp.maximum(dt, 0.0) + jnp.log1p(jnp.exp(-jnp.abs(dt)))
    rate = column_of_eight(rate_ref)
    tri = (
        lax.broadcasted_iota(jnp.int32, (T, T), 0) <= lax.broadcasted_iota(jnp.int32, (T, T), 1)
    ).astype(f32)
    cs_ref[:8, :] = lax.dot_general(
        -step * rate, tri, (((1,), (0,)), ((), ())),
        precision=lax.Precision.HIGHEST, preferred_element_type=f32,
    )
    cs_ref[8:, :] = step


def local_kernel(
    xp_ref, bcp_ref, csp_ref, taps_ref, head_ref, g1_ref, doc_ref,
    xc_ref, bcc_ref, cs_ref, msg_ref, ext_ref, dex_ref,
):
    tail = g1_ref[ROWS:, :].astype(f32)
    before = jnp.where(lax.axis_index("ctx") > 0, tail[32:48, :128], 0.0)
    ext_ref[:16, :T] = tail[:16]
    ext_ref[:16, T:] = tail[16:32]
    ext_ref[16:, :] = head_ref[:, :768]
    dex_ref[:16, :] = before
    dex_ref[16:, :] = head_ref[:, 768:]
    xc_ref[...] = xp_ref[...]
    bcc_ref[...] = bcp_ref[...]
    convolve(ext_ref, dex_ref, taps_ref, 0, 16, xc_ref, bcc_ref)
    cum, step = csp_ref[:8, :], csp_ref[8:, :]
    cs_ref[:16, :] = csp_ref[...]
    cs_ref[16:, :] = jnp.concatenate([before[8:16]] * 3, axis=1)

    row = doc_ref[...].reshape(1, T).astype(f32)
    first, last = jnp.min(row), jnp.max(row)
    cum_end = cum[:, T - 1 :]
    end_w = jnp.where(row == last, jnp.exp(cum_end - cum) * step, 0.0)
    xt = jnp.transpose(xc_ref[...].astype(f32))
    xw = (xt.reshape(MHL, PS, T) * end_w[:, None, :]).reshape(MHL * PS, T).astype(bf16)
    state = nn(xw, bcc_ref[:, :NS])
    msg_ref[:, :16, :] = state.astype(bf16).reshape(32, 16, NS)
    whole = jnp.logical_and(before[15:16] == first + 1.0, last == first).astype(f32)
    gain = jnp.exp(cum_end) * whole
    high = gain.astype(bf16).astype(f32)
    low = gain - high
    at = lax.broadcasted_iota(jnp.int32, (MHL, 16, NS), 1)
    block = jnp.where(
        at == 0, high[:, None, :], jnp.where(at == 1, low[:, None, :], 0.0)
    ).astype(bf16)
    for q in range(4):
        for h in range(MHL):
            msg_ref[h * 4 + q, 16:, :] = block[h]


def scan_kernel(msg_ref, _, out_ref):
    state = jnp.zeros((16, NS), f32)
    for j in range(32):
        out_ref[j] = state.astype(bf16)
        block = msg_ref[j].astype(f32)
        state = (block[16:17] + block[17:18]) * state + block[:16]


def intra_kernel(xc_ref, bcc_ref, cs_ref, doc_ref, skip_ref, *refs):
    y_ref, cb_ref = refs[-2:]
    skip = column_of_eight(skip_ref)
    row = doc_ref[...].reshape(1, T).astype(f32)
    own = column_of(row)
    order_t = lax.broadcasted_iota(jnp.int32, (T, T), 0)
    order_s = lax.broadcasted_iota(jnp.int32, (T, T), 1)
    allowed = (tile_lanes(own, 3) == row) & (order_s <= order_t)
    cb_ref[...] = jnp.where(allowed, nt(bcc_ref[:, NS:], bcc_ref[:, :NS]), 0.0)
    cum = cs_ref[:8, :]
    cum_t = columns_of(cum)
    late = cum - jnp.log(cs_ref[8:16, :])
    for r in range(0, T, 128):
        k = r + 128
        cb = cb_ref[r:k, :k]
        for pair in range(MHL // 2):
            halves = []
            for h in (2 * pair, 2 * pair + 1):
                gap = cum_t[r:k, h : h + 1] - late[h : h + 1, :k]
                mix = (jnp.exp(jnp.minimum(gap, 60.0)) * cb).astype(bf16)
                x = xc_ref[:k, h * PS : (h + 1) * PS]
                halves.append(nn(mix, x) + skip[h : h + 1] * x[r:k].astype(f32))
            y_ref[r:k, pair * 128 : pair * 128 + 128] = jnp.concatenate(halves, axis=1)


def deal_rows(full_ref, out_ref):
    tp = lax.axis_index("tp")
    core = lax.rem(tp, 2)
    for d, ahead in enumerate((2, 0, 1, 3)):
        base = 2 * lax.rem(tp // 2 + ahead, 4)
        mine = pl.multiple_of((base + core) * 48, 16)
        other = pl.multiple_of((base + 1 - core) * 48, 16)
        out_ref[d * 48 : d * 48 + 48, :] = full_ref[pl.ds(mine, 48), :]
        out_ref[192 + d * 48 : 240 + d * 48, :] = full_ref[pl.ds(other, 48), :]


def gated_norm(z_ref, y_ref, state_ref, bcc_ref, cs_ref, doc_ref, gain_ref, g_ref, full_ref):
    own = column_of(doc_ref[...].reshape(1, T).astype(f32) + 1.0)
    prev = cs_ref[23:24, :128]
    entry = jnp.exp(columns_of(cs_ref[:8, :])) * (own == prev).astype(f32)
    from_state = nt(bcc_ref[:, NS:], state_ref[...])
    lane = lax.broadcasted_iota(jnp.int32, (T, 128), 1)
    total = jnp.zeros((T, 1), f32)
    for pair in range(MHL // 2):
        c = slice(pair * 128, pair * 128 + 128)
        e = jnp.where(
            lane < PS, entry[:, 2 * pair : 2 * pair + 1], entry[:, 2 * pair + 1 : 2 * pair + 2]
        )
        g = (y_ref[:, c] + from_state[:, c] * e) * jax.nn.silu(z_ref[:, c].astype(f32))
        g_ref[:, c] = g
        total = total + jnp.sum(g * g, axis=1, keepdims=True)
    inverse = lax.rsqrt(total * (1.0 / (MHL * PS)) + 1e-05)
    full_ref[...] = (g_ref[...] * inverse * gain_ref[...]).astype(bf16)


def pack_kernel(k_hbm, v_hbm, x_ref, bc_ref, doc_ref, pack_ref, next_ref, k_ref, v_ref, sems):
    copies = fetch([(k_hbm, k_ref), (v_hbm, v_ref)], sems)
    row = doc_ref[...].reshape(1, T).astype(f32)
    ids = jnp.broadcast_to(row, (16, T)).astype(bf16)
    next_ref[ROWS : ROWS + 16, :] = x_ref[:, :T]
    next_ref[ROWS + 16 : ROWS + 32, :128] = x_ref[:, T:]
    next_ref[ROWS + 16 : ROWS + 32, 128:] = bc_ref[...]
    last_ids = (column_of(row)[T - 16 :] + 1.0).astype(bf16)
    next_ref[ROWS + 32 :, :] = jnp.concatenate([last_ids] * 3, axis=1)
    for copy in copies:
        copy.wait()
    keys = jnp.transpose(k_ref[...].astype(f32)).astype(bf16)
    for ref in (pack_ref, next_ref):
        ref[:HW, :] = keys
        for c in range(3):
            ref[HW : 2 * HW, c * 128 : c * 128 + 128] = v_ref[c * 128 : c * 128 + 128, :]
        ref[2 * HW : ROWS, :] = ids


def join_kernel(a_ref, b_ref, c_ref, msg_ref, up_ref, down_ref, out_ref):
    up_ref[:ROWS] = a_ref[:ROWS]
    up_ref[ROWS:] = b_ref[...]
    down_ref[:ROWS] = b_ref[...]
    down_ref[ROWS:] = c_ref[...]
    out_ref[...] = msg_ref[...]


def heads_of(q_ref, qs_ref):
    one = (lax.broadcasted_iota(jnp.int32, (T, HW), 1) == 0).astype(bf16)
    for h in range(QH):
        qs_ref[h * T : h * T + T, :HW] = q_ref[:, h * HW : (h + 1) * HW]
        qs_ref[h * T : h * T + T, HW:] = one


def fold(scores, values, m_ref, al_ref):
    s = scores(0)
    for h in range(QH):
        later = scores(h + 1) if h + 1 < QH else None
        m_old = m_ref[h]
        m_new = jnp.maximum(m_old, jnp.max(s, axis=1, keepdims=True))
        p = jnp.exp2(s * SCALE - tile_lanes(m_new * SCALE, s.shape[1] // 128)).astype(bf16)
        factor = jnp.exp2((m_old - m_new) * SCALE)
        al_ref[h] = al_ref[h] * tile_lanes(factor, 2) + nn(p, values)
        m_ref[h] = m_new
        s = later


def far_blocks(blocks, position, first, qs_ref, packs, m_ref, al_ref, k_ref, v_ref):
    n = len(blocks)
    touches, biases = False, []
    for which, base, behind in blocks:
        ids = packs[which][base + 2 * HW : base + ROWS, :].astype(f32)[:1, :]
        inside = position >= behind
        touches = touches | ((jnp.max(ids) == first) & inside)
        biases.append(jnp.where((ids == first) & inside, 0.0, LOW))

    @pl.when(touches)
    def _():
        top = lax.broadcasted_iota(jnp.int32, (16, T), 0) == 0
        for b, (which, base, _) in enumerate(blocks):
            ref = packs[which]
            c = slice(b * T, b * T + T)
            k_ref[:HW, c] = ref[base : base + HW, :]
            k_ref[HW : HW + 16, c] = jnp.where(top, biases[b], 0.0).astype(bf16)
            for i in range(3):
                row = b * T + i * 128
                v_ref[row : row + 128, :HW] = ref[base + HW : base + 2 * HW, i * 128 : i * 128 + 128]

        def scores(h):
            return nn(qs_ref[h * T : h * T + T, :], k_ref[:, : n * T])

        fold(scores, v_ref[: n * T, :], m_ref, al_ref)


def set_up(k_ref, v_ref):
    k_ref[HW:, :] = jnp.zeros((HW, k_ref.shape[1]), bf16)
    v_ref[:, HW:] = jnp.ones((v_ref.shape[0], HW), bf16)


def first_kernel(waves, n, q_hbm, own_ref, *refs):
    packs = refs[:n]
    out_ref, m_ref, al_ref, q_ref, qs_ref, kt_ref, vs_ref, sems = refs[n:]
    copies = fetch([(q_hbm, q_ref)], sems)
    row = own_ref[2 * HW :, :].astype(f32)[:1, :]
    first, last = jnp.min(row), jnp.max(row)
    position = lax.axis_index("ctx")
    m_ref[...] = jnp.full(m_ref.shape, LOW, f32)
    al_ref[...] = jnp.zeros(al_ref.shape, f32)
    set_up(kt_ref, vs_ref)
    copies[0].wait()
    heads_of(q_ref, qs_ref)
    for blocks in waves:
        far_blocks(blocks, position, first, qs_ref, packs, m_ref, al_ref, kt_ref, vs_ref)
    own = column_of(row)

    @pl.when(last != first)
    def _():
        keeps = own == first

        @pl.loop(0, QH)
        def _(h):
            m_ref[h] = jnp.where(keeps, m_ref[h], LOW)
            al_ref[h] = jnp.where(tile_lanes(keeps, 2), al_ref[h], 0.0)

    order_t = lax.broadcasted_iota(jnp.int32, (T, T), 0)
    order_s = lax.broadcasted_iota(jnp.int32, (T, T), 1)
    allowed = (tile_lanes(own, 3) == row) & (order_s <= order_t)
    for c in range(3):
        vs_ref[c * 128 : c * 128 + 128, :HW] = own_ref[HW : 2 * HW, c * 128 : c * 128 + 128]

    def scores(h):
        return jnp.where(allowed, nn(qs_ref[h * T : h * T + T, :HW], own_ref[:HW, :]), LOW)

    fold(scores, vs_ref[:T, :], m_ref, al_ref)
    half = lax.broadcasted_iota(jnp.int32, (T, 128), 1) < 64
    for h in range(QH):
        out_ref[h, :, :HW] = al_ref[h, :, :HW]
        out_ref[h, :, HW:] = jnp.where(half, al_ref[h, :, HW:], m_ref[h])


def last_kernel(waves, n, doc_ref, gain_ref, *refs):
    packs = refs[:n]
    q_hbm, al_hbm, z_hbm, y_hbm, state_hbm, bcc_hbm, cs_hbm, wa_hbm, wm_hbm = refs[n : n + 9]
    outs = refs[n + 9 : n + 15]
    (
        m_ref, al_ref, q_ref, al_in, z_ref, y_ref, state_ref, bcc_ref, cs_ref, w_ref,
        qs_ref, kt_ref, vs_ref, full_ref, g_ref, both_ref, part_ref, sems, out_sems,
    ) = refs[n + 15 :]
    copies = fetch(
        [
            (q_hbm, q_ref),
            (al_hbm, al_in),
            (z_hbm, z_ref),
            (y_hbm, y_ref),
            (state_hbm, state_ref),
            (bcc_hbm, bcc_ref),
            (cs_hbm, cs_ref),
            (wa_hbm, w_ref.at[: QH * HW]),
            (wm_hbm, w_ref.at[QH * HW :]),
        ],
        sems,
    )
    row = doc_ref[...].reshape(1, T).astype(f32)
    first, last = jnp.min(row), jnp.max(row)
    position = lax.axis_index("ctx")
    m_ref[...] = jnp.full(m_ref.shape, LOW, f32)
    al_ref[...] = jnp.zeros(al_ref.shape, f32)
    set_up(kt_ref, vs_ref)
    copies[0].wait()
    heads_of(q_ref, qs_ref)
    for blocks in waves:
        far_blocks(blocks, position, first, qs_ref, packs, m_ref, al_ref, kt_ref, vs_ref)

    for copy in copies[1:7]:
        copy.wait()
    gated_norm(z_ref, y_ref, state_ref, bcc_ref, cs_ref, doc_ref, gain_ref, g_ref, full_ref)
    deal_rows(full_ref, both_ref.at[:, QH * HW :])
    keeps = column_of(row) == first
    for h in range(QH):
        m_far = jnp.where(keeps, m_ref[h], LOW)
        m_old = jnp.broadcast_to(al_in[h, :, 192:193], (T, 128))
        m = jnp.maximum(m_far, m_old)
        far, old = jnp.exp2((m_far - m) * SCALE), jnp.exp2((m_old - m) * SCALE)
        far = jnp.where(keeps, far, 0.0)
        top = al_ref[h, :, :HW] * far + al_in[h, :, :HW] * old
        bottom = al_ref[h, :, HW:] * far + jnp.broadcast_to(al_in[h, :, HW : HW + 1], (T, 128)) * old
        full_ref[:, h * HW : (h + 1) * HW] = (top / bottom).astype(bf16)
    deal_rows(full_ref, both_ref.at[:, : QH * HW])
    for copy in copies[7:]:
        copy.wait()
    sent = []
    for j in range(0, D, COLS):
        c = pl.ds(j, COLS)
        part_ref[:, c] = nn(both_ref[...], w_ref[:, c]).astype(bf16)
        sent += fetch(
            [
                (part_ref.at[:48, c], outs[0].at[:, c]),
                (part_ref.at[48:96, c], outs[1].at[:, c]),
                (part_ref.at[96:144, c], outs[2].at[:, c]),
                (part_ref.at[144:192, c], outs[3].at[:, c]),
                (part_ref.at[192:240, c], outs[4].at[:, c]),
                (part_ref.at[240:, c], outs[5].at[:, c]),
            ],
            out_sems.at[j // COLS],
        )
    for copy in sent:
        copy.wait()


STATE = sds((QH, T, 256), f32)


def widest(waves):
    return max(len(blocks) for blocks in waves) * T


def attend_first(waves, q, pack, packs):
    n = len(packs)
    return pl.pallas_call(
        functools.partial(first_kernel, waves, n),
        out_shape=STATE,
        in_specs=[HBM] + [VMEM] * (n + 1),
        out_specs=VMEM,
        scratch_shapes=[
            pltpu.VMEM((QH, T, 128), f32),
            pltpu.VMEM((QH, T, 256), f32),
            pltpu.VMEM((T, QH * HW), bf16),
            pltpu.VMEM((QH * T, 2 * HW), bf16),
            pltpu.VMEM((2 * HW, widest(waves)), bf16),
            pltpu.VMEM((widest(waves), 2 * HW), bf16),
            pltpu.SemaphoreType.DMA((1,)),
        ],
        compiler_params=params(60),
        cost_estimate=cost(*COSTS["attend_first"]),
        name="attend_first",
    )(q, pack, *packs)


def attend_last(waves, doc_row, gain, packs, *arrays):
    n = len(packs)
    pieces = [sds((48, D), bf16)] * 5 + [sds((144, D), bf16)]
    depth = QH * HW + MHL * PS
    return pl.pallas_call(
        functools.partial(last_kernel, waves, n),
        out_shape=pieces,
        in_specs=[VMEM] * (n + 2) + [HBM] * 9,
        out_specs=[HBM] * 6,
        scratch_shapes=[
            pltpu.VMEM((QH, T, 128), f32),
            pltpu.VMEM((QH, T, 256), f32),
            *[pltpu.VMEM(a.shape, a.dtype) for a in arrays[:7]],
            pltpu.VMEM((depth, D), bf16),
            pltpu.VMEM((QH * T, 2 * HW), bf16),
            pltpu.VMEM((2 * HW, widest(waves)), bf16),
            pltpu.VMEM((widest(waves), 2 * HW), bf16),
            pltpu.VMEM((T, QH * HW), bf16),
            pltpu.VMEM((T, MHL * PS), f32),
            pltpu.VMEM((T, depth), bf16),
            pltpu.VMEM((T, D), bf16),
            pltpu.SemaphoreType.DMA((9,)),
            pltpu.SemaphoreType.DMA((D // COLS, 6)),
        ],
        compiler_params=params(58),
        cost_estimate=cost(*COSTS["attend_last"]),
        name="attend_last",
    )(doc_row, gain, *packs, *arrays)


SPLIT = 3072


def far_kernel(keep_ref, got_ref, a_ref, b_ref):
    total = keep_ref[...].astype(f32) + got_ref[...].astype(f32)
    a_ref[...] = total[:, :SPLIT].astype(bf16)
    b_ref[...] = total[:, SPLIT:].astype(bf16)


def far_sum(keep, got):
    return pl.pallas_call(
        far_kernel,
        out_shape=[sds((48, SPLIT), bf16), sds((48, D - SPLIT), bf16)],
        in_specs=[VMEM] * 2,
        out_specs=[VMEM] * 2,
        compiler_params=params(8),
        cost_estimate=cost(*COSTS["combine"]),
        name="far_sum",
    )(keep, got)


def cores_kernel(own_ref, up_ref, down_ref, got_ref, *outs):
    for i, ref in enumerate((own_ref, up_ref, down_ref)):
        outs[i][...] = ref[...].astype(f32) + got_ref[48 * i : 48 * i + 48].astype(f32)


def cores_sum(own, up, down, got):
    return pl.pallas_call(
        cores_kernel,
        out_shape=[sds((48, D), f32)] * 3,
        in_specs=[VMEM] * 4,
        out_specs=[VMEM] * 3,
        compiler_params=params(8),
        cost_estimate=cost(*COSTS["combine"]),
        name="cores_sum",
    )(own, up, down, got)


def near_kernel(at, near_ref, far_ref, out_ref):
    out_ref[...] = near_ref[...].astype(bf16)
    c = slice(at, at + far_ref.shape[1])
    out_ref[:, c] = (near_ref[:, c] + far_ref[...].astype(f32)).astype(bf16)


def near_sum(near, far, at):
    return pl.pallas_call(
        functools.partial(near_kernel, at),
        out_shape=sds((48, D), bf16),
        in_specs=[VMEM] * 2,
        out_specs=VMEM,
        compiler_params=params(8),
        cost_estimate=cost(*COSTS["combine"]),
        name="near_sum",
    )(near, far)


def along(v, by):
    n = lax.axis_size("ctx")
    return lax.ppermute(v, "ctx", [(i, (i + by) % n) for i in range(n)])


def from_previous(v):
    n = lax.axis_size("ctx")
    return lax.ppermute(v, "ctx", [(i, i + 1) for i in range(n - 1)])


def along_y(v, by):
    return lax.ppermute(
        v, "tp", [(2 * y + c, 2 * ((y + by) % 4) + c) for y in range(4) for c in range(2)]
    )


def other_core(v):
    return lax.ppermute(v, "tp", [(i, i ^ 1) for i in range(8)])


def body(
    query, key, value, doc_ids, mamba_x, mamba_bc, gate_z, dt_raw, decay_rate,
    conv_x, conv_bc, skip_gain, norm_gain, attn_out_weight, mamba_out_weight,
):
    doc_row = doc_ids
    bc = mamba_bc.reshape(T, 2 * NS)

    end = T // 16 - 1

    pack, onward = pl.pallas_call(
        pack_kernel,
        grid=(1,),
        out_shape=[sds((ROWS, T), bf16), sds((ROWS + 48, T), bf16)],
        in_specs=[
            HBM,
            HBM,
            pl.BlockSpec((16, MHL * PS), lambda i: (end, 0)),
            pl.BlockSpec((16, 2 * NS), lambda i: (end, 0)),
            VMEM,
        ],
        out_specs=[VMEM] * 2,
        scratch_shapes=[pltpu.VMEM((T, HW), bf16)] * 2 + [pltpu.SemaphoreType.DMA((2,))],
        compiler_params=params(60),
        cost_estimate=cost(*COSTS["pack"]),
        name="pack",
    )(key, value, mamba_x, bc, doc_row)
    g1 = along(onward, 1)
    g8 = along(pack, 8)
    g16 = along(pack, 16)

    prepared = pl.pallas_call(
        prepare_kernel,
        out_shape=[
            sds((T, MHL * PS), bf16), sds((T, 2 * NS), bf16), sds((16, T), f32),
            sds((KW, 768), f32), sds((16, 896), f32),
        ],
        in_specs=[HBM] * 4 + [VMEM] * 3,
        out_specs=[VMEM] * 5,
        scratch_shapes=[
            pltpu.VMEM((T + 16, 768), f32),
            pltpu.VMEM((T + 16, 128), f32),
            pltpu.VMEM((T, MHL * PS), bf16),
            pltpu.VMEM((MHL, T), f32),
            pltpu.VMEM((KW, MHL * PS), f32),
            pltpu.VMEM((MHL,), f32),
            pltpu.SemaphoreType.DMA((4,)),
        ],
        compiler_params=params(12),
        cost_estimate=cost(*COSTS["prepare"]),
        name="prepare",
    )(mamba_x, dt_raw, conv_x, decay_rate, bc, doc_row, conv_bc.reshape(KW, 2 * NS))
    xc, bcc, cs, msg = pl.pallas_call(
        local_kernel,
        out_shape=[
            sds((T, MHL * PS), bf16), sds((T, 2 * NS), bf16), sds((24, T), f32),
            sds((32, 32, NS), bf16),
        ],
        in_specs=[VMEM] * 7,
        out_specs=[VMEM] * 4,
        scratch_shapes=[pltpu.VMEM((32, 768), f32), pltpu.VMEM((32, 128), f32)],
        compiler_params=params(12),
        cost_estimate=cost(*COSTS["local"]),
        name="local",
    )(*prepared, g1, doc_row)

    up, down, msg = pl.pallas_call(
        join_kernel,
        out_shape=[sds((2 * ROWS, T), bf16)] * 2 + [sds((32, 32, NS), bf16)],
        in_specs=[VMEM] * 4,
        out_specs=[VMEM] * 3,
        compiler_params=params(12),
        cost_estimate=cost(*COSTS["join"]),
        name="join",
    )(g1, g8, g16, msg)

    msg = lax.all_to_all(msg.reshape(32 * 32, NS), "ctx", 0, 0, tiled=True)

    c29 = along(up, 1)
    c715 = along(down, -1)
    g17 = along(g16, 1)

    y = pl.pallas_call(
        intra_kernel,
        out_shape=sds((T, MHL * PS), f32),
        in_specs=[VMEM] * 5 + [ANY] * 3,
        out_specs=VMEM,
        scratch_shapes=[pltpu.VMEM((T, T), f32)],
        compiler_params=params(12),
        cost_estimate=cost(*COSTS["intra"]),
        name="intra",
    )(xc, bcc, cs, doc_row, skip_gain, c29, c715, g17)

    carried = pl.pallas_call(
        scan_kernel,
        out_shape=sds((32, 16, NS), bf16),
        in_specs=[VMEM, ANY],
        out_specs=VMEM,
        cost_estimate=cost(*COSTS["scan"]),
        compiler_params=params(8),
        name="scan",
    )(msg.reshape(32, 32, NS), y)
    carried = lax.all_to_all(carried.reshape(32 * 16, NS), "ctx", 0, 0, tiled=True)

    c310 = along(c29, 1)
    c614 = along(c715, -1)
    state = attend_first(
        [
            [(0, 0, 1), (1, 0, 8), (2, 0, 16), (3, 0, 2), (3, ROWS, 9), (4, 0, 7)],
            [(4, ROWS, 15), (5, 0, 17), (6, 0, 3), (6, ROWS, 10), (7, 0, 6), (7, ROWS, 14)],
        ],
        query, pack, [g1, g8, g16, c29, c715, g17, c310, c614],
    )
    c411 = along(c310, 1)
    c513 = along(c614, -1)
    g12 = along(c310[:ROWS], 9)

    keep_far, keep_own, keep_up, keep_down, send_far, send = attend_last(
        [[(0, 0, 4), (0, ROWS, 11), (1, 0, 5), (1, ROWS, 13), (2, 0, 12)]],
        doc_row, norm_gain.reshape(1, MHL * PS), [c411, c513, g12],
        query, state, gate_z, y, carried, bcc, cs, attn_out_weight, mamba_out_weight,
    )
    far_a, far_b = far_sum(keep_far, other_core(send_far))
    own, up, down = cores_sum(keep_own, keep_up, keep_down, other_core(send))
    up = along_y(near_sum(up, along_y(far_a, 1), 0), 1)
    down = along_y(near_sum(down, along_y(far_b, -1), SPLIT), -1)
    return (own + up.astype(f32) + down.astype(f32)).astype(bf16)


def solution(mesh):
    return jax.shard_map(
        body,
        mesh=mesh,
        in_specs=(
            P("ctx", "tp"), P("ctx", "tp"), P("ctx", "tp"), P("ctx"), P("ctx", "tp"),
            P("ctx", None, "tp"), P("ctx", "tp"), P("tp", "ctx"), P("tp"), P(None, "tp"),
            P(None, None, "tp"), P("tp"), P("tp"), P("tp", None), P("tp", None),
        ),
        out_specs=P(("ctx", "tp"), None),
        check_vma=False,
    )
```
